512 devices in a mesh: ab: 16 (over z, x_hi), ij: 16 (over y, core), rep: 2 (over x_lo).
Axes of the slice: x: 4 (x_hi: 2, x_lo: 2; x = x_hi * 2 + x_lo), y: 8, z: 8, core: 2. Of those that a mesh axis runs over, the one named last changes fastest.
Arguments:
- cholesky_a: bfloat16 [512, 64, 4096], P(('rep', 'ab'), None, 'ij'), parts along dimension 0, may hold values from -0.75 to 0.75
- cholesky_b: bfloat16 [24, 64, 4096], P('rep', None, 'ij'), parts along dimension 0, may hold values from -0.75 to 0.75
- amplitudes: bfloat16 [64, 64, 4096], P('ab', None, 'ij'), may hold values from -0.09375 to 0.09375
- other_terms: float32 [512, 12, 4096], P(('rep', 'ab'), None, 'ij'), parts along dimension 0, may hold values from -6 to 6
- virtual_a: float32 [512], P(('rep', 'ab')), parts along dimension 0, may hold values from 0.2 to 2
- virtual_b: float32 [24], P('rep'), parts along dimension 0, may hold values from 0.2 to 2
- pair_energy: float32 [4096], P('ij'), may hold values from -1.5 to -0.2
Outputs:
- residual: float32 [512, 12, 4096], P(('rep', 'ab'), None, 'ij'), parts along dimension 0
- update: float32 [512, 12, 4096], P(('rep', 'ab'), None, 'ij'), parts along dimension 0
The draws below stay inside these ranges and needn't reach their ends.
There are 2 independent parts, one for each index of `rep`. The reference program is written for one: setup_inputs(seed, part) draws one part's arguments, and reference() takes and returns one part's arrays. A program takes and returns all parts, laid end to end along the dimension named above; an argument that names none is the same for every part. Nothing has to cross between parts.
All inputs are finite; a program needn't handle non-finite values.
Results may differ from the reference program's by a relative error of at most 0.014.
Values may be sent and summed in bfloat16 or wider, within the bound.
A program may use at most 64 MiB of HBM per device.

```python
import jax
import jax.numpy as jnp

NB = 12
NC = 64
ND = 64
NP = 4096
NA = 256
IJ = 4096


def levels(rng, shape, split, smallest, top_value):
    level = 1.0
    for position, shards_of in split:
        draws = jax.random.uniform(jax.random.fold_in(jax.random.fold_in(rng, 6), position), (shards_of,), jnp.float32, smallest / len(split), top_value / len(split))
        level = level * jnp.repeat(jnp.exp(draws), shape[position] // shards_of).reshape((-1,) + (1,) * (len(shape) - 1 - position))
    return level


def centred(rng, shape, deviation, reach, cuts=(), kind=jnp.bfloat16):
    result = deviation * jax.random.normal(rng, shape, jnp.float32)
    if cuts:
        result = result * levels(rng, shape, cuts, -0.22, 0.18)
    return jnp.clip(result, -reach, reach).astype(kind)


def setup_inputs(seed: int = 0, part: int = 0) -> dict:
    key_of = jax.random.split(jax.random.key(seed), 8)
    part_splits = jax.random.split(jax.random.fold_in(key_of[7], part), 8)
    cholesky_a = centred(part_splits[0], (NA, NC, NP), 0.125, 0.75, ((0, 16), (2, 16)))
    cholesky_b = centred(part_splits[1], (NB, ND, NP), 0.125, 0.75, ((2, 16),))
    amplitudes = centred(key_of[2], (NC, ND, IJ), (NC * ND) ** -0.5, 0.09375, ((0, 16), (2, 16)))
    other_terms = centred(part_splits[3], (NA, NB, IJ), 1.0, 6.0, ((0, 16), (2, 16)), jnp.float32)
    virtual_a = jnp.clip(0.2 + 1.8 * jax.random.uniform(part_splits[4], (NA,), jnp.float32) ** levels(part_splits[4], (NA,), ((0, 16),), -0.2, 0.2), 0.2, 2.0)
    virtual_b = jnp.clip(jax.random.uniform(part_splits[5], (NB,), jnp.float32, 0.2, 2.0), 0.2, 2.0)
    pair_energy = jnp.clip(-1.5 + 1.3 * jax.random.uniform(key_of[6], (IJ,), jnp.float32) ** levels(key_of[6], (IJ,), ((0, 16),), -0.2, 0.2), -1.5, -0.2)
    return dict(cholesky_a=cholesky_a, cholesky_b=cholesky_b, amplitudes=amplitudes, other_terms=other_terms, virtual_a=virtual_a, virtual_b=virtual_b, pair_energy=pair_energy)


def reference(cholesky_a, cholesky_b, amplitudes, other_terms, virtual_a, virtual_b, pair_energy):
    left = cholesky_a.reshape(NA * NC, NP)
    right = cholesky_b.reshape(NB * ND, NP)
    integrals = jnp.dot(left, right.T, preferred_element_type=jnp.float32).astype(jnp.bfloat16)
    ordered = integrals.reshape(NA, NC, NB, ND).transpose(0, 2, 1, 3).reshape(NA * NB, NC * ND)
    ladder = jnp.dot(ordered, amplitudes.reshape(NC * ND, IJ), preferred_element_type=jnp.float32)
    residual = other_terms + ladder.reshape(NA, NB, IJ)
    divisor = virtual_a[:, None, None] + virtual_b[None, :, None] - pair_energy[None, None, :]
    return residual, residual / divisor
```

```python
import functools

import jax
import jax.numpy as jnp
from jax import lax
from jax.experimental import pallas as pl
from jax.experimental.pallas import tpu as pltpu
from jax.sharding import PartitionSpec as P

MESH = pl.DeviceIdType.MESH
BF16, F32 = jnp.bfloat16, jnp.float32
RING = 8
LONG = {1: 0, -1: 1}


def dot(a, b, dims):
    return lax.dot_general(a, b, (dims, ((), ())), preferred_element_type=F32)


def kernel(n_msg, a_hbm, b_hbm, t_hbm, out_ref,
           a_own, a_sib, b_own, b_sib, a_perm, part, rs_in, rs_out, gath, t_all, acc,
           send_sem, recv_sem, load_sem):
    ab, ij, lo = lax.axis_index("ab"), lax.axis_index("ij"), lax.axis_index("rep")
    z, hi = ab // 2, ab % 2
    y, core = ij // 2, ij % 2
    sibling = (ab, y * 2 + 1 - core, lo)
    y_next = {s: (ab, ((y + s + RING) % RING) * 2 + core, lo) for s in (1, -1)}
    z_next = {s: (((z + s + RING) % RING) * 2 + hi, ij, lo) for s in (1, -1)}
    x_far = (z * 2 + 1 - hi, ij, 1 - lo)
    x_near = (ab, ij, 1 - lo)

    started, ids = [], {}

    def send(name, src, dst, device):
        number = ids.setdefault(name, len(ids))
        copy = pltpu.make_async_remote_copy(
            src_ref=src, dst_ref=dst, send_sem=send_sem.at[number], recv_sem=recv_sem.at[number],
            device_id=device, device_id_type=MESH,
        )
        copy.start()
        started.append(copy)
        arrivals[name] = copy

    arrivals = {}

    def arrived(name):
        arrivals[name].wait_recv()

    half_a = pl.ds(pl.multiple_of(core * 32, 32), 32)
    other_half_a = pl.ds(pl.multiple_of(32 - core * 32, 32), 32)
    load_a = pltpu.make_async_copy(a_hbm.at[:, half_a], a_own, load_sem.at[0])
    load_b = pltpu.make_async_copy(b_hbm, b_own, load_sem.at[1])
    load_t = pltpu.make_async_copy(t_hbm, t_all.at[ab], load_sem.at[2])
    load_a.start()
    load_b.start()
    load_t.start()

    barrier = pltpu.get_barrier_semaphore()
    friends = (sibling, y_next[1], y_next[-1], z_next[1], z_next[-1], x_far, x_near)
    for friend in friends:
        pl.semaphore_signal(barrier, inc=1, device_id=friend, device_id_type=MESH)
    pl.semaphore_wait(barrier, len(friends))

    send("a", a_hbm.at[:, other_half_a], a_sib, sibling)
    send("b", b_hbm, b_sib, sibling)

    def t_rows(half):
        return pl.ds(half * 128, 128)

    t_far = pl.ds(pl.multiple_of((1 - lo) * 128, 128), 128)
    t_near = pl.ds(pl.multiple_of(lo * 128, 128), 128)

    def t_send_z(s, stage, half):
        slab = ((z - s * stage + 2 * RING) % RING) * 2 + hi
        src = t_hbm.at[t_rows(half)] if stage == 0 else t_all.at[slab, t_rows(half)]
        send(("z", s, stage, half), src, t_all.at[slab, t_rows(half)], z_next[s])

    def t_send_far(offset):
        slab = ((z + offset + RING) % RING) * 2 + hi
        src = t_hbm.at[t_far] if offset == 0 else t_all.at[slab, t_far]
        send(("far", offset), src, t_all.at[slab, t_far], x_far)

    def t_send_near(offset):
        arrived(("far", offset))
        slab = ((z + offset + RING) % RING) * 2 + 1 - hi
        send(("near", offset), t_all.at[slab, t_near], t_all.at[slab, t_near], x_near)

    def t_stage(stage):
        for s in (1, -1):
            arrived(("z", s, stage, LONG[s]))
            if stage < 3:
                t_send_z(s, stage + 1, LONG[s])
        if stage < 3:
            for s in (1, -1):
                arrived(("z", s, stage, 1 - LONG[s]))
                if stage < 2:
                    t_send_z(s, stage + 1, 1 - LONG[s])
                t_send_far(-s * (stage + 1))
        else:
            t_send_far(4)

    for s in (1, -1):
        t_send_z(s, 0, LONG[s])
    t_send_far(0)
    for s in (1, -1):
        t_send_z(s, 0, 1 - LONG[s])

    row = lax.broadcasted_iota(jnp.int32, (256, 256), 0)
    column = lax.broadcasted_iota(jnp.int32, (256, 256), 1)
    swap = jnp.where(column == (row % 16) * 16 + row // 16, 1.0, 0.0).astype(BF16)

    def reorder(ref, place):
        for block in range(2):
            rows = ref[:, block * 16:(block + 1) * 16, :].reshape(256, 256)
            a_perm[place, block * 256:(block + 1) * 256, :] = dot(swap, rows, ((1,), (0,))).astype(BF16)

    load_a.wait()
    reorder(a_own, 0)
    load_b.wait()
    part[...] = dot(a_perm[0], b_own[...], ((1,), (1,)))
    arrived("a")
    reorder(a_sib, 1)
    arrived("b")
    part[...] += dot(a_perm[1], b_sib[...], ((1,), (1,)))

    def rs_slot(s, stage, half):
        long = half == LONG[s]
        return (0 if s == 1 else 7) + (stage if long else 4 + stage)

    def rs_send(s, stage, half):
        distance = (4 if half == LONG[s] else 3) - stage
        owner = (y + s * distance + RING) % RING
        rows = pl.ds(pl.multiple_of(owner * 64 + half * 32, 32), 32)
        value = part[rows, :]
        if stage:
            arrived(("rs", s, stage - 1, half))
            value = value + rs_in[rs_slot(s, stage - 1, half)].astype(F32)
        slot = rs_slot(s, stage, half)
        rs_out[slot] = value.astype(BF16)
        send(("rs", s, stage, half), rs_out.at[slot], rs_in.at[slot], y_next[s])

    def rs_stage(stage):
        for s in (1, -1):
            rs_send(s, stage, LONG[s])
        if stage < 3:
            for s in (1, -1):
                rs_send(s, stage, 1 - LONG[s])

    rs_stage(0)
    t_stage(0)
    rs_stage(1)
    t_send_near(0)
    t_stage(1)
    rs_stage(2)
    for offset in (-1, 1):
        t_send_near(offset)
    t_stage(2)
    rs_stage(3)

    me = core * RING + y
    total = []
    for half in range(2):
        value = part[pl.ds(pl.multiple_of(y * 64 + half * 32, 32), 32), :]
        for s in (1, -1):
            last = 3 if half == LONG[s] else 2
            arrived(("rs", s, last, half))
            value = value + rs_in[rs_slot(s, last, half)].astype(F32)
        total.append(value)
    total = jnp.concatenate(total, axis=0)
    for b in range(12):
        block = jnp.concatenate([total[c * 16:(c + 1) * 16, b * 64:(b + 1) * 64] for c in range(4)], axis=1)
        gath[me, b * 16:(b + 1) * 16, :] = block.astype(BF16)

    def g_rows(half):
        return pl.ds(half * 96, 96)

    def g_send(s, stage, half):
        slab = core * RING + (y - s * stage + RING) % RING
        ref = gath.at[slab, g_rows(half)]
        send(("g", s, stage, half), ref, ref, y_next[s])

    def g_sib(offset):
        slab = core * RING + (y + offset + RING) % RING
        send(("gs", offset), gath.at[slab], gath.at[slab], sibling)

    def ladder(offset, other):
        slab = (1 - core if other else core) * RING + (y + offset + RING) % RING
        return dot(gath[slab], t_all[slab], ((1,), (0,)))

    for s in (1, -1):
        g_send(s, 0, LONG[s])
    for s in (1, -1):
        g_send(s, 0, 1 - LONG[s])
    g_sib(0)

    for offset in (-2, 2):
        t_send_near(offset)
    t_stage(3)
    for offset in (-3, 3, 4):
        t_send_near(offset)

    for stage in range(4):
        for s in (1, -1):
            arrived(("g", s, stage, LONG[s]))
            if stage < 3:
                g_send(s, stage + 1, LONG[s])
        if stage < 3:
            for s in (1, -1):
                arrived(("g", s, stage, 1 - LONG[s]))
                if stage < 2:
                    g_send(s, stage + 1, 1 - LONG[s])
                g_sib(-s * (stage + 1))
        else:
            g_sib(4)
        if stage == 0:
            load_t.wait()
            for offset in (0, -1, 1, -2, 2, -3, 3, 4):
                arrived(("near", offset))
            acc[...] = ladder(0, False)
        if stage < 3:
            acc[...] += ladder(-stage - 1, False) + ladder(stage + 1, False)
        else:
            acc[...] += ladder(4, False)
        for offset in ((0,), (-1, 1), (-2, 2), (-3, 3))[stage]:
            arrived(("gs", offset))
            acc[...] += ladder(offset, True)
    arrived(("gs", 4))
    out_ref[...] = acc[...] + ladder(4, True)

    for copy in started:
        copy.wait_send()
    assert len(ids) == n_msg


def shards(cholesky_a, cholesky_b, amplitudes, other_terms, virtual_a, virtual_b, pair_energy):
    n_msg = 2 + 14 + 8 + 8 + 14 + 14 + 8
    any_spec = pl.BlockSpec(memory_space=pl.ANY)
    ladder = pl.pallas_call(
        functools.partial(kernel, n_msg),
        out_shape=jax.ShapeDtypeStruct((192, 256), F32),
        in_specs=[any_spec] * 3,
        out_specs=pl.BlockSpec(memory_space=pltpu.VMEM),
        scratch_shapes=[
            pltpu.VMEM((16, 32, 256), BF16),
            pltpu.VMEM((16, 32, 256), BF16),
            pltpu.VMEM((768, 256), BF16),
            pltpu.VMEM((768, 256), BF16),
            pltpu.VMEM((2, 512, 256), BF16),
            pltpu.VMEM((512, 768), F32),
            pltpu.VMEM((14, 32, 768), BF16),
            pltpu.VMEM((14, 32, 768), BF16),
            pltpu.VMEM((16, 192, 256), BF16),
            pltpu.VMEM((16, 256, 256), BF16),
            pltpu.VMEM((192, 256), F32),
            pltpu.SemaphoreType.DMA((n_msg,)),
            pltpu.SemaphoreType.DMA((n_msg,)),
            pltpu.SemaphoreType.DMA((3,)),
        ],
        compiler_params=pltpu.CompilerParams(
            collective_id=0, has_side_effects=True, vmem_limit_bytes=40 * 2**20
        ),
        cost_estimate=pl.CostEstimate(flops=2 * 512 * 512 * 768 + 2 * 192 * 4096 * 256, bytes_accessed=2**21, transcendentals=0),
    )(cholesky_a, cholesky_b.reshape(768, 256), amplitudes.reshape(256, 256))
    ladder = ladder.reshape(12, 16, 256).transpose(1, 0, 2)
    residual = other_terms + ladder
    divisor = virtual_a[:, None, None] + virtual_b[None, :, None] - pair_energy[None, None, :]
    return (residual, residual / divisor)


def solution(mesh):
    return jax.shard_map(
        shards,
        mesh=mesh,
        in_specs=(
            P(("rep", "ab"), None, "ij"),
            P("rep", None, "ij"),
            P("ab", None, "ij"),
            P(("rep", "ab"), None, "ij"),
            P(("rep", "ab")),
            P("rep"),
            P("ij"),
        ),
        out_specs=(P(("rep", "ab"), None, "ij"), P(("rep", "ab"), None, "ij")),
        check_vma=False,
    )
```

```python
import jax
import jax.numpy as jnp
from jax import lax
from jax.experimental import pallas as pl
from jax.experimental.pallas import tpu as pltpu
from jax.sharding import PartitionSpec as P

MESH = pl.DeviceIdType.MESH
BF16, F32 = jnp.bfloat16, jnp.float32
RING = 8
PIECES = 4
LONG = {1: (0, 1), -1: (2, 3)}
SHORT = {1: (2, 3), -1: (0, 1)}
T_LONG = {1: 0, -1: 1}
N_RECV, N_SEND = 68, 8


def dot(a, b, dims):
    return lax.dot_general(a, b, (dims, ((), ())), preferred_element_type=F32)


def rotation(pieces):
    return [(s, pieces[s][i]) for i in range(PIECES // 2) for s in (1, -1)]


def kernel(a_hbm, b_hbm, t_hbm, va_hbm, vb_hbm, pe_hbm, out_ref, div_ref,
           va_ref, vb_ref, pe_ref, a_in, a_all, b_all, part, rs_in, rs_out, gath, t_all,
           send_sem, recv_sem, load_sem):
    ab, ij, lo = lax.axis_index("ab"), lax.axis_index("ij"), lax.axis_index("rep")
    z, hi = ab // 2, ab % 2
    y, core = ij // 2, ij % 2
    sibling = (ab, y * 2 + 1 - core, lo)
    y_next = {s: (ab, ((y + s + RING) % RING) * 2 + core, lo) for s in (1, -1)}
    z_next = {s: (((z + s + RING) % RING) * 2 + hi, ij, lo) for s in (1, -1)}
    x_far = (z * 2 + 1 - hi, ij, 1 - lo)
    x_near = (ab, ij, 1 - lo)
    x_near_sibling = (ab, y * 2 + 1 - core, 1 - lo)

    numbers = ({}, {})

    def recv_of(to, name):
        return recv_sem.at[numbers[to].setdefault(name, len(numbers[to]))]

    def send(to, name, src, dst, device, group):
        pltpu.make_async_remote_copy(
            src_ref=src, dst_ref=dst, send_sem=send_sem.at[group], recv_sem=recv_of(to, name),
            device_id=device, device_id_type=MESH,
        ).start()

    def arrived(to, name, ref):
        pltpu.make_async_remote_copy(
            src_ref=ref, dst_ref=ref, send_sem=send_sem.at[0], recv_sem=recv_of(to, name),
            device_id=sibling, device_id_type=MESH,
        ).wait_recv()

    def sent(group, ref):
        pltpu.make_async_remote_copy(
            src_ref=ref, dst_ref=ref, send_sem=send_sem.at[group], recv_sem=recv_sem.at[0],
            device_id=sibling, device_id_type=MESH,
        ).wait_send()

    def meet(friends):
        barrier = pltpu.get_barrier_semaphore()
        for friend in friends:
            pl.semaphore_signal(barrier, inc=1, device_id=friend, device_id_type=MESH)
        pl.semaphore_wait(barrier, len(friends))

    load_a = pltpu.make_async_copy(a_hbm, a_in, load_sem.at[0])
    load_b = pltpu.make_async_copy(b_hbm, b_all.at[:, 0:256], load_sem.at[1])
    load_t = pltpu.make_async_copy(t_hbm, t_all.at[core, ab], load_sem.at[2])
    loads_small = [
        pltpu.make_async_copy(src, dst, load_sem.at[3 + i])
        for i, (src, dst) in enumerate(((va_hbm, va_ref), (vb_hbm, vb_ref), (pe_hbm, pe_ref)))
    ]
    for load in (load_a, load_b, load_t, *loads_small):
        load.start()

    row = lax.broadcasted_iota(jnp.int32, (256, 256), 0)
    column = lax.broadcasted_iota(jnp.int32, (256, 256), 1)
    swap = jnp.where(column == (row % 16) * 16 + row // 16, 1.0, 0.0).astype(BF16)

    def block_of(k):
        return ((y + 4) // 2 + k) % 4

    def reorder(k):
        block = block_of(k)
        rows = a_in[:, pl.ds(pl.multiple_of(block * 16, 16), 16), :].reshape(256, 256)
        place = pl.ds(pl.multiple_of(block * 256, 256), 256)
        a_all[place, 0:256] = dot(swap, rows, ((1,), (0,))).astype(BF16)
        return place

    def divisor():
        for load in loads_small:
            load.wait()
        eye = lax.broadcasted_iota(jnp.int32, (16, 16), 0) == lax.broadcasted_iota(jnp.int32, (16, 16), 1)
        va = jnp.sum(jnp.where(eye, jnp.broadcast_to(va_ref[...], (16, 16)), 0.0), axis=1, keepdims=True)
        for b in range(12):
            div_ref[b * 16:(b + 1) * 16, :] = (va + vb_ref[0:1, b:b + 1]) - pe_ref[...]

    def ladder(offset):
        slab = (y + offset + RING) % RING
        left = jnp.concatenate([gath[slab, p] for p in range(PIECES)], axis=1)
        right = t_all[core, pl.ds(2 * slab, 2)].reshape(512, 256)
        return dot(left, right, ((1,), (0,)))

    def early_ladder():
        out_ref[...] = ladder(0)
        for offset in (1, -1, 2, -2, 3, -3):
            out_ref[...] += ladder(offset)

    def core0():
        meet((sibling, z_next[1], z_next[-1], x_far, x_near, x_near_sibling))
        send(1, "b", b_hbm, b_all.at[:, 256:512], sibling, 0)

        def half_rows(half):
            return pl.ds(half * 128, 128)

        t_far = pl.ds(pl.multiple_of((1 - lo) * 128, 128), 128)
        t_near = pl.ds(pl.multiple_of(lo * 128, 128), 128)

        def own(offset):
            return ((z + offset + RING) % RING) * 2 + hi

        def other(offset):
            return ((z + offset + RING) % RING) * 2 + 1 - hi

        def first(col):
            src = t_hbm if col == 0 else t_all.at[1, ab]
            for halves in ((0, 1), (1, 0)):
                for s, half in zip((1, -1), halves):
                    rows = half_rows(half)
                    send(0, ("z", s, 0, half, col), src.at[rows], t_all.at[col, ab, rows], z_next[s], 2)
                if halves == (0, 1):
                    send(0, ("far", 0, col), src.at[t_far], t_all.at[col, ab, t_far], x_far, 3)

        def z_arrived(s, stage, half):
            slab, rows = own(-s * (stage + 1)), half_rows(half)
            if stage == 0:
                for col in range(2):
                    arrived(0, ("z", s, 0, half, col), t_all.at[col, slab, rows])
            else:
                arrived(0, ("z", s, stage, half), t_all.at[:, slab, rows])
            if stage < (3 if half == T_LONG[s] else 2):
                ref = t_all.at[:, slab, rows]
                send(0, ("z", s, stage + 1, half), ref, ref, z_next[s], 2)

        def spread(offset):
            slab = own(offset)
            ref = t_all.at[:, slab] if offset == 4 else t_all.at[:, slab, t_far]
            send(0, ("far", offset), ref, ref, x_far, 3)
            send(1, "t", t_all.at[1, slab], t_all.at[1, slab], sibling, 5)

        def near(offset):
            slab = other(offset)
            if offset == 0:
                for col in range(2):
                    arrived(0, ("far", 0, col), t_all.at[col, slab, t_near])
            else:
                arrived(0, ("far", offset), t_all.at[:, slab, t_near])
            ref0, ref1 = t_all.at[0, slab, t_near], t_all.at[1, slab, t_near]
            send(0, "near", ref0, ref0, x_near, 4)
            send(1, "t", ref1, ref1, x_near_sibling, 4)
            send(1, "t", ref1, ref1, sibling, 6)

        first(0)
        load_a.wait()
        for k in range(4):
            place = reorder(k)
            send(1, ("a", k), a_all.at[place, 0:256], a_all.at[place, 256:512], sibling, 1)
        arrived(0, "t", t_all.at[1, ab])
        first(1)
        divisor()
        load_b.wait()
        load_t.wait()
        for stage in range(4):
            for s in (1, -1):
                z_arrived(s, stage, T_LONG[s])
            if stage < 3:
                for s in (1, -1):
                    z_arrived(s, stage, 1 - T_LONG[s])
                    spread(-s * (stage + 1))
            else:
                spread(4)
            for offset in ((0,), (-1, 1), (-2, 2), (-3, 3))[stage]:
                near(offset)
        slab = other(4)
        arrived(0, ("far", 4), t_all.at[:, slab])
        send(1, "t", t_all.at[1, slab], t_all.at[1, slab], sibling, 7)
        arrived(0, "near", t_all.at[0, 0:7, 0:128])

        arrived(0, "g early", gath.at[0:7])
        early_ladder()
        arrived(0, "g last", gath.at[0])
        out_ref[...] += ladder(4)

        sent(0, b_all.at[:, 0:256])
        sent(1, a_all.at[:, 0:256])
        sent(2, t_all.at[0, 0:14])
        sent(3, t_all.at[0, 0:9])
        sent(4, t_all.at[0, 0:7])
        sent(5, t_all.at[0, 0:7])
        sent(6, t_all.at[0, 0:7, 0:128])
        sent(7, t_all.at[0, 0])

    def core1():
        meet((sibling, y_next[1], y_next[-1], x_near_sibling))
        send(0, "t", t_hbm, t_all.at[1, ab], sibling, 0)
        load_a.wait()
        for k in range(4):
            reorder(k)
        load_b.wait()
        arrived(1, "b", b_all.at[:, 256:512])
        for k in range(4):
            arrived(1, ("a", k), a_all.at[pl.ds(pl.multiple_of(block_of(k) * 256, 256), 256), 256:512])

        def chunk(offset):
            rows = pl.ds(pl.multiple_of(((y + offset + RING) % RING) * 128, 128), 128)
            part[rows, :] = dot(a_all[rows, :], b_all[...], ((1,), (1,)))

        slots = {}

        def own_part(offset, piece):
            chip = (y + offset + RING) % RING
            return part[pl.ds(pl.multiple_of(chip * 128 + piece * 32, 32), 32), :]

        def received(s, stage, piece):
            slot = slots[s, stage, piece]
            arrived(1, ("rs", s, stage, piece), rs_in.at[slot])
            return rs_in[slot].astype(F32)

        def rs_send(s, stage, piece):
            value = own_part(s * ((4 if piece in LONG[s] else 3) - stage), piece)
            if stage:
                value = value + received(s, stage - 1, piece)
            slot = slots.setdefault((s, stage, piece), len(slots))
            rs_out[slot] = value.astype(BF16)
            send(1, ("rs", s, stage, piece), rs_out.at[slot], rs_in.at[slot], y_next[s], 1)

        chunk(4)
        for s, piece in rotation(LONG):
            rs_send(s, 0, piece)
        chunk(3)
        chunk(-3)
        for s, piece in rotation(SHORT):
            rs_send(s, 0, piece)
        chunk(2)
        chunk(-2)
        for stage in (1, 2, 3):
            for s, piece in rotation(LONG):
                rs_send(s, stage, piece)
            if stage < 3:
                for s, piece in rotation(SHORT):
                    rs_send(s, stage, piece)
            if stage == 1:
                chunk(1)
                chunk(-1)
                chunk(0)

        def slab_of(offset):
            return (y + offset + RING) % RING

        def g_send(s, stage, piece):
            ref = gath.at[slab_of(-s * stage), piece]
            send(1, ("g", s, stage, piece), ref, ref, y_next[s], 2)

        def g_arrived(s, stage, piece):
            arrived(1, ("g", s, stage, piece), gath.at[slab_of(-s * (stage + 1)), piece])
            if stage < (3 if piece in LONG[s] else 2):
                g_send(s, stage + 1, piece)

        def g_hand(offset):
            ref = gath.at[slab_of(offset)]
            send(0, "g last" if offset == 4 else "g early", ref, ref, sibling, 3)

        for _, piece in rotation(LONG):
            value = own_part(0, piece)
            for s in (1, -1):
                value = value + received(s, 3 if piece in LONG[s] else 2, piece)
            for b in range(12):
                block = jnp.concatenate([value[c * 16:(c + 1) * 16, b * 64:(b + 1) * 64] for c in range(2)], axis=1)
                gath[y, piece, b * 16:(b + 1) * 16, :] = block.astype(BF16)
            for s in (1, -1):
                g_send(s, 0, piece)
        g_hand(0)
        for stage in range(3):
            for s, piece in rotation(LONG):
                g_arrived(s, stage, piece)
            for s, piece in rotation(SHORT):
                g_arrived(s, stage, piece)
            for s in (1, -1):
                g_hand(-s * (stage + 1))
        divisor()
        load_t.wait()
        arrived(1, "t", t_all.at[1, 0:15])
        early_ladder()
        for s, piece in rotation(LONG):
            g_arrived(s, 3, piece)
        g_hand(4)
        out_ref[...] += ladder(4)

        sent(0, t_all.at[1, 0])
        sent(1, rs_out)
        sent(2, gath.at[0:7])
        sent(3, gath)

    pl.when(core == 0)(core0)
    pl.when(core == 1)(core1)
    assert max(map(len, numbers)) <= N_RECV


def shards(cholesky_a, cholesky_b, amplitudes, other_terms, virtual_a, virtual_b, pair_energy):
    hbm = pl.BlockSpec(memory_space=pltpu.HBM)
    vmem = pl.BlockSpec(memory_space=pltpu.VMEM)
    result = jax.ShapeDtypeStruct((192, 256), F32)
    ladder, divisor = pl.pallas_call(
        kernel,
        out_shape=(result, result),
        in_specs=[hbm] * 6,
        out_specs=(vmem, vmem),
        scratch_shapes=[
            pltpu.VMEM((1, 16), F32),
            pltpu.VMEM((1, 12), F32),
            pltpu.VMEM((1, 256), F32),
            pltpu.VMEM((16, 64, 256), BF16),
            pltpu.VMEM((1024, 512), BF16),
            pltpu.VMEM((768, 512), BF16),
            pltpu.VMEM((1024, 768), F32),
            pltpu.VMEM((28, 32, 768), BF16),
            pltpu.VMEM((28, 32, 768), BF16),
            pltpu.VMEM((8, PIECES, 192, 128), BF16),
            pltpu.VMEM((2, 16, 256, 256), BF16),
            pltpu.SemaphoreType.DMA((N_SEND,)),
            pltpu.SemaphoreType.DMA((N_RECV,)),
            pltpu.SemaphoreType.DMA((6,)),
        ],
        compiler_params=pltpu.CompilerParams(
            collective_id=0, has_side_effects=True, vmem_limit_bytes=40 * 2**20
        ),
        cost_estimate=pl.CostEstimate(flops=2 * 1024 * 512 * 768 + 2 * 192 * 4096 * 256, bytes_accessed=2**21, transcendentals=0),
    )(
        *(
            pltpu.with_memory_space_constraint(operand, pltpu.HBM)
            for operand in (
                cholesky_a, cholesky_b.reshape(768, 256), amplitudes.reshape(256, 256),
                virtual_a.reshape(1, 16), virtual_b.reshape(1, 12), pair_energy.reshape(1, 256),
            )
        )
    )
    residual = other_terms + ladder.reshape(12, 16, 256).transpose(1, 0, 2)
    return (residual, residual / divisor.reshape(12, 16, 256).transpose(1, 0, 2))


def solution(mesh):
    return jax.shard_map(
        shards,
        mesh=mesh,
        in_specs=(
            P(("rep", "ab"), None, "ij"),
            P("rep", None, "ij"),
            P("ab", None, "ij"),
            P(("rep", "ab"), None, "ij"),
            P(("rep", "ab")),
            P("rep"),
            P("ij"),
        ),
        out_specs=(P(("rep", "ab"), None, "ij"), P(("rep", "ab"), None, "ij")),
        check_vma=False,
    )
```

```python
import jax
import jax.numpy as jnp
from jax import lax
from jax.experimental import pallas as pl
from jax.experimental.pallas import tpu as pltpu
from jax.sharding import PartitionSpec as P

MESH = pl.DeviceIdType.MESH
BF16, F32 = jnp.bfloat16, jnp.float32
RING = 8
PIECES = 4
LONG = {1: (0, 1), -1: (2, 3)}
SHORT = {1: (2, 3), -1: (0, 1)}
N_RECV, N_SEND = 68, 8


def dot(a, b, dims):
    return lax.dot_general(a, b, (dims, ((), ())), preferred_element_type=F32)


def rotation(pieces):
    return [(s, pieces[s][i]) for i in range(PIECES // 2) for s in (1, -1)]


def kernel(a_hbm, b_hbm, t_hbm, va_hbm, vb_hbm, pe_hbm, out_ref, div_ref,
           va_ref, vb_ref, pe_ref, a_in, a_all, b_all, part, rs_in, rs_out, gath, t_all,
           send_sem, recv_sem, load_sem, go_sem, ready_sem):
    ab, ij, lo = lax.axis_index("ab"), lax.axis_index("ij"), lax.axis_index("rep")
    z, hi = ab // 2, ab % 2
    y, core = ij // 2, ij % 2
    sibling = (ab, y * 2 + 1 - core, lo)
    y_next = {s: (ab, ((y + s + RING) % RING) * 2 + core, lo) for s in (1, -1)}
    z_hop = {s: (((z + s + RING) % RING) * 2 + hi, ij, lo) for s in (1, -1)}
    x_far = (z * 2 + 1 - hi, ij, 1 - lo)
    x_near = (ab, ij, 1 - lo)
    x_near_sibling = (ab, y * 2 + 1 - core, 1 - lo)

    numbers = ({}, {})

    def recv_of(to, name):
        return recv_sem.at[numbers[to].setdefault(name, len(numbers[to]))]

    def send(to, name, src, dst, device, group):
        pltpu.make_async_remote_copy(
            src_ref=src, dst_ref=dst, send_sem=send_sem.at[group], recv_sem=recv_of(to, name),
            device_id=device, device_id_type=MESH,
        ).start()

    def arrived(to, name, ref):
        pltpu.make_async_remote_copy(
            src_ref=ref, dst_ref=ref, send_sem=send_sem.at[0], recv_sem=recv_of(to, name),
            device_id=sibling, device_id_type=MESH,
        ).wait_recv()

    def sent(group, ref):
        pltpu.make_async_remote_copy(
            src_ref=ref, dst_ref=ref, send_sem=send_sem.at[group], recv_sem=recv_sem.at[0],
            device_id=sibling, device_id_type=MESH,
        ).wait_send()

    load_a = pltpu.make_async_copy(a_hbm, a_in, load_sem.at[0])
    load_b = pltpu.make_async_copy(b_hbm, b_all.at[:, 0:256], load_sem.at[1])
    load_t = pltpu.make_async_copy(t_hbm, t_all.at[core, ab], load_sem.at[2])
    loads_small = [
        pltpu.make_async_copy(src, dst, load_sem.at[3 + i])
        for i, (src, dst) in enumerate(((va_hbm, va_ref), (vb_hbm, vb_ref), (pe_hbm, pe_ref)))
    ]

    barrier = pltpu.get_barrier_semaphore()

    def enter(friends):
        for friend in friends:
            pl.semaphore_signal(barrier, inc=1, device_id=friend, device_id_type=MESH)
        for load in (load_a, load_b, load_t, *loads_small):
            load.start()

    row = lax.broadcasted_iota(jnp.int32, (256, 256), 0)
    column = lax.broadcasted_iota(jnp.int32, (256, 256), 1)
    swap = jnp.where(column == (row % 16) * 16 + row // 16, 1.0, 0.0).astype(BF16)

    def block_of(k):
        return ((y + 4) // 2 + k) % 4

    def reorder(k):
        block = block_of(k)
        rows = a_in[:, pl.ds(pl.multiple_of(block * 16, 16), 16), :].reshape(256, 256)
        place = pl.ds(pl.multiple_of(block * 256, 256), 256)
        a_all[place, 0:256] = dot(swap, rows, ((1,), (0,))).astype(BF16)
        return place

    def divisor():
        for load in loads_small:
            load.wait()
        eye = lax.broadcasted_iota(jnp.int32, (16, 16), 0) == lax.broadcasted_iota(jnp.int32, (16, 16), 1)
        va = jnp.sum(jnp.where(eye, jnp.broadcast_to(va_ref[...], (16, 16)), 0.0), axis=1, keepdims=True)
        for b in range(12):
            div_ref[b * 16:(b + 1) * 16, :] = (va + vb_ref[0:1, b:b + 1]) - pe_ref[...]

    def ladder(offset):
        slab = (y + offset + RING) % RING
        left = jnp.concatenate([gath[slab, p] for p in range(PIECES)], axis=1)
        right = t_all[core, pl.ds(2 * slab, 2)].reshape(512, 256)
        return dot(left, right, ((1,), (0,)))

    def early_ladder():
        out_ref[...] = ladder(0)
        for offset in (1, -1, 2, -2, 3, -3):
            out_ref[...] += ladder(offset)

    def core0():
        friends = (*z_hop.values(), x_far, x_near)
        enter((sibling, *friends))
        load_a.wait()
        places = [reorder(k) for k in range(4)]
        pl.semaphore_wait(go_sem, 1)
        send(1, "b", b_hbm, b_all.at[:, 256:512], sibling, 0)

        def rows_of(piece):
            return pl.ds(piece * 64, 64)

        def rows_x(pair, side):
            return pl.ds(pl.multiple_of(pair * 128 + side * 64, 64), 64)

        def own(offset):
            return ((z + offset + RING) % RING) * 2 + hi

        def other(offset):
            return ((z + offset + RING) % RING) * 2 + 1 - hi

        def first(col):
            src = t_hbm if col == 0 else t_all.at[1, ab]
            for pieces in (LONG, SHORT):
                for s, piece in rotation(pieces):
                    rows = rows_of(piece)
                    send(0, ("z", s, 1, piece), src.at[rows], t_all.at[col, ab, rows], z_hop[s], 2)
                if pieces is LONG:
                    for pair in range(2):
                        rows = rows_x(pair, 1 - lo)
                        send(0, ("far", 0, pair), src.at[rows], t_all.at[col, ab, rows], x_far, 3)

        def z_arrived(s, distance, piece):
            slab, rows = own(-s * distance), rows_of(piece)
            ref = t_all.at[:, slab, rows]
            arrived(0, ("z", s, distance, piece), ref)
            if distance < (4 if piece in LONG[s] else 3):
                send(0, ("z", s, distance + 1, piece), ref, ref, z_hop[s], 2)
            send(1, "t", t_all.at[1, slab, rows], t_all.at[1, slab, rows], sibling, 5)

        def z_pair(s, distance, pieces):
            offset = 4 if distance == 4 else -s * distance
            pair = pieces[s][0] // 2
            rows = pl.ds(pair * 128, 128) if offset == 4 else rows_x(pair, 1 - lo)
            ref = t_all.at[:, own(offset), rows]
            send(0, ("far", offset, pair), ref, ref, x_far, 3)

        def near(offset, pair):
            slab, rows = other(offset), rows_x(pair, lo)
            arrived(0, ("far", offset, pair), t_all.at[:, slab, rows])
            ref0, ref1 = t_all.at[0, slab, rows], t_all.at[1, slab, rows]
            send(0, "near", ref0, ref0, x_near, 4)
            send(1, "t", ref1, ref1, x_near_sibling, 4)
            send(1, "t", ref1, ref1, sibling, 6)

        for k, place in enumerate(places):
            send(1, "a rest" if k else "a first", a_all.at[place, 0:256], a_all.at[place, 256:512], sibling, 1)
        pl.semaphore_wait(barrier, len(friends))
        first(0)
        pl.semaphore_signal(ready_sem, inc=1, device_id=x_near, device_id_type=MESH)
        arrived(0, "t", t_all.at[1, ab])
        first(1)
        load_b.wait()
        load_t.wait()
        divisor()
        for distance in (1, 2, 3, 4):
            for pieces in (LONG, SHORT) if distance < 4 else (LONG,):
                for s, piece in rotation(pieces):
                    z_arrived(s, distance, piece)
                for s in (1, -1):
                    z_pair(s, distance, pieces)
            if distance == 1:
                pl.semaphore_wait(ready_sem, 1)
                for pair in range(2):
                    near(0, pair)
            else:
                for s, pair in ((1, 0), (-1, 1), (1, 1), (-1, 0)):
                    near(-s * (distance - 1), pair)
        for pair in range(2):
            slab, rows = other(4), pl.ds(pair * 128, 128)
            arrived(0, ("far", 4, pair), t_all.at[:, slab, rows])
            send(1, "t", t_all.at[1, slab, rows], t_all.at[1, slab, rows], sibling, 7)
        arrived(0, "near", t_all.at[0, 0:7, 0:128])

        arrived(0, "g early", gath.at[0:7])
        early_ladder()
        arrived(0, "g last", gath.at[0])
        out_ref[...] += ladder(4)

        sent(0, b_all.at[:, 0:256])
        sent(1, a_all.at[:, 0:256])
        sent(2, t_all.at[0, 0:14])
        sent(3, t_all.at[0, 0:9])
        sent(4, t_all.at[0, 0:7])
        sent(5, t_all.at[0, 0:7])
        sent(6, t_all.at[0, 0:7, 0:128])
        sent(7, t_all.at[0, 0])

    def core1():
        enter(y_next.values())
        pl.semaphore_wait(barrier, 3)
        pl.semaphore_signal(go_sem, inc=1, device_id=sibling, device_id_type=MESH)
        send(0, "t", t_hbm, t_all.at[1, ab], sibling, 0)
        def chunk_rows(offset):
            return pl.ds(pl.multiple_of(((y + offset + RING) % RING) * 128, 128), 128)

        def add_sibling(*offsets):
            left = jnp.concatenate([a_all[chunk_rows(offset), 256:512] for offset in offsets], axis=0)
            product = dot(left, b_all[:, 256:512], ((1,), (1,)))
            for i, offset in enumerate(offsets):
                part[chunk_rows(offset), :] += product[i * 128:(i + 1) * 128]

        slots = {}

        def own_part(offset, piece):
            chip = (y + offset + RING) % RING
            return part[pl.ds(pl.multiple_of(chip * 128 + piece * 32, 32), 32), :]

        def received(s, stage, piece):
            slot = slots[s, stage, piece]
            arrived(1, ("rs", s, stage, piece), rs_in.at[slot])
            return rs_in[slot].astype(F32)

        def rs_send(s, stage, piece):
            value = own_part(s * ((4 if piece in LONG[s] else 3) - stage), piece)
            if stage:
                value = value + received(s, stage - 1, piece)
            slot = slots.setdefault((s, stage, piece), len(slots))
            rs_out[slot] = value.astype(BF16)
            send(1, ("rs", s, stage, piece), rs_out.at[slot], rs_in.at[slot], y_next[s], 1)

        def rs_stage(stage, pieces):
            for s, piece in rotation(pieces):
                rs_send(s, stage, piece)

        load_a.wait()
        for k in range(4):
            reorder(k)
        load_b.wait()
        for rows in (slice(0, 512), slice(512, 1024)):
            part[rows, :] = dot(a_all[rows, 0:256], b_all[:, 0:256], ((1,), (1,)))
        arrived(1, "b", b_all.at[:, 256:512])
        arrived(1, "a first", a_all.at[0:256, 256:512])
        add_sibling(4)
        rs_stage(0, LONG)
        arrived(1, "a rest", a_all.at[0:768, 256:512])
        add_sibling(3, -3)
        rs_stage(0, SHORT)
        add_sibling(2, -2)
        rs_stage(1, LONG)
        rs_stage(1, SHORT)
        add_sibling(1, -1)
        rs_stage(2, LONG)
        rs_stage(2, SHORT)
        add_sibling(0)
        rs_stage(3, LONG)

        def slab_of(offset):
            return (y + offset + RING) % RING

        def g_send(s, stage, piece):
            ref = gath.at[slab_of(-s * stage), piece]
            send(1, ("g", s, stage, piece), ref, ref, y_next[s], 2)

        def g_arrived(s, stage, piece):
            offset = -s * (stage + 1)
            arrived(1, ("g", s, stage, piece), gath.at[slab_of(offset), piece])
            if stage < (3 if piece in LONG[s] else 2):
                g_send(s, stage + 1, piece)
            g_hand(offset, piece)

        def g_hand(offset, piece):
            ref = gath.at[slab_of(offset), piece]
            send(0, "g last" if abs(offset) == 4 else "g early", ref, ref, sibling, 3)

        for way, piece in rotation(LONG):
            value = own_part(0, piece)
            for s in (1, -1):
                value = value + received(s, 3 if piece in LONG[s] else 2, piece)
            for b in range(12):
                block = jnp.concatenate([value[c * 16:(c + 1) * 16, b * 64:(b + 1) * 64] for c in range(2)], axis=1)
                gath[y, piece, b * 16:(b + 1) * 16, :] = block.astype(BF16)
            g_send(way, 0, piece)
        for s, piece in rotation(SHORT):
            g_send(s, 0, piece)
        for piece in range(PIECES):
            g_hand(0, piece)
        for stage in range(3):
            for pieces in (LONG, SHORT):
                for s, piece in rotation(pieces):
                    g_arrived(s, stage, piece)
        divisor()
        load_t.wait()
        arrived(1, "t", t_all.at[1, 0:15])
        early_ladder()
        for s, piece in rotation(LONG):
            g_arrived(s, 3, piece)
        out_ref[...] += ladder(4)

        sent(0, t_all.at[1, 0])
        sent(1, rs_out)
        sent(2, gath.at[0:7])
        sent(3, gath)

    pl.when(core == 1)(core1)
    pl.when(core == 0)(core0)
    assert max(map(len, numbers)) <= N_RECV


def shards(cholesky_a, cholesky_b, amplitudes, other_terms, virtual_a, virtual_b, pair_energy):
    hbm = pl.BlockSpec(memory_space=pltpu.HBM)
    vmem = pl.BlockSpec(memory_space=pltpu.VMEM)
    result = jax.ShapeDtypeStruct((192, 256), F32)
    ladder, divisor = pl.pallas_call(
        kernel,
        out_shape=(result, result),
        in_specs=[hbm] * 6,
        out_specs=(vmem, vmem),
        scratch_shapes=[
            pltpu.VMEM((1, 16), F32),
            pltpu.VMEM((1, 12), F32),
            pltpu.VMEM((1, 256), F32),
            pltpu.VMEM((16, 64, 256), BF16),
            pltpu.VMEM((1024, 512), BF16),
            pltpu.VMEM((768, 512), BF16),
            pltpu.VMEM((1024, 768), F32),
            pltpu.VMEM((28, 32, 768), BF16),
            pltpu.VMEM((28, 32, 768), BF16),
            pltpu.VMEM((8, PIECES, 192, 128), BF16),
            pltpu.VMEM((2, 16, 256, 256), BF16),
            pltpu.SemaphoreType.DMA((N_SEND,)),
            pltpu.SemaphoreType.DMA((N_RECV,)),
            pltpu.SemaphoreType.DMA((6,)),
            pltpu.SemaphoreType.REGULAR,
            pltpu.SemaphoreType.REGULAR,
        ],
        compiler_params=pltpu.CompilerParams(
            collective_id=0, has_side_effects=True, vmem_limit_bytes=40 * 2**20
        ),
        cost_estimate=pl.CostEstimate(flops=2 * 1024 * 512 * 768 + 2 * 192 * 4096 * 256, bytes_accessed=2**21, transcendentals=0),
    )(
        *(
            pltpu.with_memory_space_constraint(operand, pltpu.HBM)
            for operand in (
                cholesky_a, cholesky_b.reshape(768, 256), amplitudes.reshape(256, 256),
                virtual_a.reshape(1, 16), virtual_b.reshape(1, 12), pair_energy.reshape(1, 256),
            )
        )
    )
    residual = other_terms + ladder.reshape(12, 16, 256).transpose(1, 0, 2)
    return (residual, residual / divisor.reshape(12, 16, 256).transpose(1, 0, 2))


def solution(mesh):
    return jax.shard_map(
        shards,
        mesh=mesh,
        in_specs=(
            P(("rep", "ab"), None, "ij"),
            P("rep", None, "ij"),
            P("ab", None, "ij"),
            P(("rep", "ab"), None, "ij"),
            P(("rep", "ab")),
            P("rep"),
            P("ij"),
        ),
        out_specs=(P(("rep", "ab"), None, "ij"), P(("rep", "ab"), None, "ij")),
        check_vma=False,
    )
```

```python
import jax
import jax.numpy as jnp
from jax import lax
from jax.experimental import pallas as pl
from jax.experimental.pallas import tpu as pltpu
from jax.sharding import PartitionSpec as P

MESH = pl.DeviceIdType.MESH
BF16, F32 = jnp.bfloat16, jnp.float32
RING = 8
PIECES = 4
LONG = {1: (0, 1), -1: (2, 3)}
SHORT = {1: (2, 3), -1: (0, 1)}
N_RECV, N_SEND = 50, 7


SLOTS = {
    key: i for i, key in enumerate(
        (s, stage, piece) for s in (1, -1) for stage in range(4) for piece in LONG[s] + (SHORT[s] if stage < 3 else ())
    )
}


def dot(a, b, dims):
    return lax.dot_general(a, b, (dims, ((), ())), preferred_element_type=F32)


def rotation(pieces, ways=(1, -1)):
    return [(s, pieces[s][i]) for i in range(PIECES // 2) for s in ways]


def kernel(a_hbm, b_hbm, t_hbm, va_hbm, vb_hbm, pe_hbm, out_ref, div_ref,
           va_ref, vb_ref, pe_ref, a_in, a_all, b_all, part, part_0, rs_in, rs_out, gath, t_all,
           send_sem, recv_sem, load_sem, go_sem, ready_sem):
    ab, ij, lo = lax.axis_index("ab"), lax.axis_index("ij"), lax.axis_index("rep")
    z, hi = ab // 2, ab % 2
    y, core = ij // 2, ij % 2
    sibling = (ab, y * 2 + 1 - core, lo)
    y_next = {s: (ab, ((y + s + RING) % RING) * 2 + core, lo) for s in (1, -1)}
    z_hop = {s: (((z + s + RING) % RING) * 2 + hi, ij, lo) for s in (1, -1)}
    x_far = (z * 2 + 1 - hi, ij, 1 - lo)
    x_near = (ab, ij, 1 - lo)
    x_near_sibling = (ab, y * 2 + 1 - core, 1 - lo)

    numbers = ({}, {})

    def recv_of(to, name):
        if name[0] == "g":
            name = ("rs", *name[1:])
        return recv_sem.at[numbers[to].setdefault(name, len(numbers[to]))]

    def send(to, name, src, dst, device, group):
        pltpu.make_async_remote_copy(
            src_ref=src, dst_ref=dst, send_sem=send_sem.at[group], recv_sem=recv_of(to, name),
            device_id=device, device_id_type=MESH,
        ).start()

    def arrived(to, name, ref):
        pltpu.make_async_remote_copy(
            src_ref=ref, dst_ref=ref, send_sem=send_sem.at[0], recv_sem=recv_of(to, name),
            device_id=sibling, device_id_type=MESH,
        ).wait_recv()

    def sent(group, ref):
        pltpu.make_async_remote_copy(
            src_ref=ref, dst_ref=ref, send_sem=send_sem.at[group], recv_sem=recv_sem.at[0],
            device_id=sibling, device_id_type=MESH,
        ).wait_send()

    load_a = pltpu.make_async_copy(a_hbm, a_in, load_sem.at[0])
    load_b = pltpu.make_async_copy(b_hbm, b_all, load_sem.at[1])
    load_t = pltpu.make_async_copy(t_hbm, t_all.at[core, ab], load_sem.at[2])
    loads_small = [
        pltpu.make_async_copy(src, dst, load_sem.at[3 + i])
        for i, (src, dst) in enumerate(((va_hbm, va_ref), (vb_hbm, vb_ref), (pe_hbm, pe_ref)))
    ]

    barrier = pltpu.get_barrier_semaphore()

    def enter(friends):
        for friend in friends:
            pl.semaphore_signal(barrier, inc=1, device_id=friend, device_id_type=MESH)
        for load in (load_a, load_b, load_t, *loads_small):
            load.start()

    row = lax.broadcasted_iota(jnp.int32, (256, 256), 0)
    column = lax.broadcasted_iota(jnp.int32, (256, 256), 1)
    swap = jnp.where(column == (row % 16) * 16 + row // 16, 1.0, 0.0).astype(BF16)

    def block_of(k):
        return ((y + 4) // 2 + k) % 4

    def reorder(k):
        block = block_of(k)
        rows = a_in[:, pl.ds(pl.multiple_of(block * 16, 16), 16), :].reshape(256, 256)
        place = pl.ds(pl.multiple_of(block * 256, 256), 256)
        a_all[place, :] = dot(swap, rows, ((1,), (0,))).astype(BF16)

    def chunk_rows(offset):
        return pl.ds(pl.multiple_of(((y + offset + RING) % RING) * 128, 128), 128)

    def products(ref, *offsets):
        left = jnp.concatenate([a_all[chunk_rows(offset), :] for offset in offsets], axis=0)
        value = dot(left, b_all[...], ((1,), (1,))).astype(ref.dtype)
        for i, offset in enumerate(offsets):
            ref[chunk_rows(offset), :] = value[i * 128:(i + 1) * 128]

    def divisor():
        for load in loads_small:
            load.wait()
        eye = lax.broadcasted_iota(jnp.int32, (16, 16), 0) == lax.broadcasted_iota(jnp.int32, (16, 16), 1)
        va = jnp.sum(jnp.where(eye, jnp.broadcast_to(va_ref[...], (16, 16)), 0.0), axis=1, keepdims=True)
        for b in range(12):
            div_ref[b * 16:(b + 1) * 16, :] = (va + vb_ref[0:1, b:b + 1]) - pe_ref[...]

    far_y = (y + 4) % RING
    far_z = jnp.where(z == y, (y + 5) % RING, (z + 4) % RING)
    low, high = jnp.minimum(far_y, far_z), jnp.maximum(far_y, far_z)

    def ladder(slabs):
        total = None
        for slab in slabs:
            left = jnp.concatenate([gath[slab, p] for p in range(PIECES)], axis=1)
            right = t_all[core, pl.ds(2 * slab, 2)].reshape(512, 256)
            product = dot(left, right, ((1,), (0,)))
            total = product if total is None else total + product
        return total

    def early_ladder():
        slabs = []
        for k in range(RING - 2):
            slab = k + jnp.where(k >= low, 1, 0)
            slabs.append(slab + jnp.where(slab >= high, 1, 0))
        out_ref[...] = ladder(slabs)

    def late_ladder():
        out_ref[...] += ladder((far_y, far_z))

    def core0():
        friends = (*z_hop.values(), x_far, x_near)
        enter((sibling, *friends))

        def hand_products(*offsets):
            products(part_0, *offsets)
            if offsets == (4,):
                pl.semaphore_wait(go_sem, 1)
            for offset in offsets:
                ref = part_0.at[chunk_rows(offset)]
                send(1, ("p", offsets[0]), ref, ref, sibling, 0)

        load_a.wait()
        reorder(0)
        load_b.wait()
        hand_products(4)
        for k in (1, 3, 2):
            reorder(k)
        hand_products(3, -3)

        def rows_x(pair, side):
            return pl.ds(pl.multiple_of(pair * 128 + side * 64, 64), 64)

        def rows_of(piece):
            return rows_x(piece // 2, lo if piece % 2 else 1 - lo)

        def own(offset):
            return ((z + offset + RING) % RING) * 2 + hi

        def other(offset):
            return ((z + offset + RING) % RING) * 2 + 1 - hi

        def z_send(s, distance, piece):
            ref = t_all.at[:, own(-s * (distance - 1)), rows_of(piece)]
            send(0, ("z", s, distance, piece), ref, ref, z_hop[s], 2)

        def far_send(offset, piece):
            name = ("far", offset, piece if offset == 4 else piece // 2)
            ref = t_all.at[:, own(offset), rows_of(piece)]
            send(0, name, ref, ref, x_far, 3)

        def z_arrived(s, distance, piece):
            slab, rows = own(-s * distance), rows_of(piece)
            arrived(0, ("z", s, distance, piece), t_all.at[:, slab, rows])
            if distance < (4 if piece in LONG[s] else 3):
                z_send(s, distance + 1, piece)
            if distance == 4:
                far_send(4, piece)
            elif piece % 2 == 0:
                far_send(-s * distance, piece)
            send(1, "t", t_all.at[1, slab, rows], t_all.at[1, slab, rows], sibling, 5)

        def near(offset, pair):
            slab, rows = other(offset), rows_x(pair, lo)
            arrived(0, ("far", offset, pair), t_all.at[:, slab, rows])
            ref0, ref1 = t_all.at[0, slab, rows], t_all.at[1, slab, rows]
            send(0, "near", ref0, ref0, x_near, 4)
            send(1, "t", ref1, ref1, x_near_sibling, 4)
            send(1, "t", ref1, ref1, sibling, 6)

        pl.semaphore_wait(barrier, len(friends))
        pl.semaphore_signal(ready_sem, inc=1, device_id=x_near, device_id_type=MESH)
        load_t.wait()
        arrived(0, "t", t_all.at[1, ab])
        for s, piece in rotation(LONG):
            z_send(s, 1, piece)
        for pair in range(2):
            far_send(0, 2 * pair)
        for s, piece in rotation(SHORT):
            z_send(s, 1, piece)
        hand_products(2, -2)
        hand_products(1, -1)
        hand_products(0)
        divisor()
        for distance in (1, 2, 3, 4):
            for pieces in (LONG, SHORT) if distance < 4 else (LONG,):
                for s, piece in rotation(pieces):
                    z_arrived(s, distance, piece)
            if distance == 1:
                pl.semaphore_wait(ready_sem, 1)
                for pair in range(2):
                    near(0, pair)
            else:
                for s, pair in ((1, 0), (-1, 1), (1, 1), (-1, 0)):
                    near(-s * (distance - 1), pair)
        slab = other(4)
        for _, piece in rotation(LONG):
            rows = rows_x(piece // 2, 1 - lo if piece % 2 else lo)
            arrived(0, ("far", 4, piece), t_all.at[:, slab, rows])
            send(1, "t last", t_all.at[1, slab, rows], t_all.at[1, slab, rows], sibling, 1)
        arrived(0, "near", t_all.at[0, 0:7, 0:128])

        arrived(0, "g early", gath.at[0:7])
        early_ladder()
        arrived(0, "g last", gath.at[0])
        late_ladder()

        sent(0, part_0)
        sent(1, t_all.at[0, 0])
        sent(2, t_all.at[0, 0:14])
        sent(3, t_all.at[0, 0:9])
        sent(4, t_all.at[0, 0:7])
        sent(5, t_all.at[0, 0:7])
        sent(6, t_all.at[0, 0:7, 0:128])

    def core1(ways):
        enter(y_next.values())
        pl.semaphore_wait(barrier, 3)
        pl.semaphore_signal(go_sem, inc=1, device_id=sibling, device_id_type=MESH)
        send(0, "t", t_hbm, t_all.at[1, ab], sibling, 0)

        def own_part(offset, piece):
            chip = (y + offset + RING) % RING
            rows = pl.ds(pl.multiple_of(chip * 128 + piece * 32, 32), 32)
            return part[rows, :] + part_0[rows, :].astype(F32)

        def received(s, stage, piece):
            slot = SLOTS[s, stage, piece]
            arrived(1, ("rs", s, stage, piece), rs_in.at[slot])
            return rs_in[slot].astype(F32)

        def rs_send(s, stage, piece):
            value = own_part(s * ((4 if piece in LONG[s] else 3) - stage), piece)
            if stage:
                value = value + received(s, stage - 1, piece)
            slot = SLOTS[s, stage, piece]
            rs_out[slot] = value.astype(BF16)
            send(1, ("rs", s, stage, piece), rs_out.at[slot], rs_in.at[slot], y_next[s], 1)

        def rs_stage(stage, pieces):
            for s, piece in rotation(pieces, ways):
                rs_send(s, stage, piece)

        load_a.wait()
        for k in range(4):
            reorder(k)
        load_b.wait()
        products(part, 4)
        products(part, 3, -3)
        products(part, 2, -2)
        arrived(1, ("p", 4), part_0.at[0:128])
        rs_stage(0, LONG)
        arrived(1, ("p", 3), part_0.at[0:256])
        rs_stage(0, SHORT)
        products(part, 1, -1)
        products(part, 0)
        rs_stage(1, LONG)
        arrived(1, ("p", 2), part_0.at[0:256])
        rs_stage(1, SHORT)
        rs_stage(2, LONG)
        arrived(1, ("p", 1), part_0.at[0:256])
        rs_stage(2, SHORT)
        rs_stage(3, LONG)
        arrived(1, ("p", 0), part_0.at[0:128])

        def slab_of(offset):
            return (y + offset + RING) % RING

        def g_send(s, stage, piece):
            ref = gath.at[slab_of(-s * stage), piece]
            send(1, ("g", s, stage, piece), ref, ref, y_next[s], 2)

        def g_arrived(s, stage, piece):
            offset = -s * (stage + 1)
            arrived(1, ("g", s, stage, piece), gath.at[slab_of(offset), piece])
            if stage < (3 if piece in LONG[s] else 2):
                g_send(s, stage + 1, piece)
            g_hand(offset, piece)

        def g_hand(offset, piece):
            ref = gath.at[slab_of(offset), piece]
            send(0, "g last" if abs(offset) == 4 else "g early", ref, ref, sibling, 3)

        for way, piece in rotation(LONG, ways):
            value = own_part(0, piece)
            for s in (1, -1):
                value = value + received(s, 3 if piece in LONG[s] else 2, piece)
            for b in range(12):
                block = jnp.concatenate([value[c * 16:(c + 1) * 16, b * 64:(b + 1) * 64] for c in range(2)], axis=1)
                gath[y, piece, b * 16:(b + 1) * 16, :] = block.astype(BF16)
            g_send(way, 0, piece)
        for s, piece in rotation(SHORT, ways):
            g_send(s, 0, piece)
        for piece in range(PIECES):
            g_hand(0, piece)
        for stage in range(3):
            for pieces in (LONG, SHORT):
                for s, piece in rotation(pieces, ways):
                    g_arrived(s, stage, piece)
        divisor()
        load_t.wait()
        for s, piece in rotation(LONG, ways):
            g_arrived(s, 3, piece)
        arrived(1, "t", t_all.at[1, 0:14])
        early_ladder()
        arrived(1, "t last", t_all.at[1, 0])
        late_ladder()

        sent(0, t_all.at[1, 0])
        sent(1, rs_out)
        sent(2, gath.at[0:7])
        sent(3, gath)

    pl.when((core == 1) & (y % 4 < 2))(lambda: core1((-1, 1)))
    pl.when((core == 1) & (y % 4 >= 2))(lambda: core1((1, -1)))
    pl.when(core == 0)(core0)
    assert max(map(len, numbers)) <= N_RECV


def shards(cholesky_a, cholesky_b, amplitudes, other_terms, virtual_a, virtual_b, pair_energy):
    hbm = pl.BlockSpec(memory_space=pltpu.HBM)
    vmem = pl.BlockSpec(memory_space=pltpu.VMEM)
    result = jax.ShapeDtypeStruct((192, 256), F32)
    ladder, divisor = pl.pallas_call(
        kernel,
        out_shape=(result, result),
        in_specs=[hbm] * 6,
        out_specs=(vmem, vmem),
        scratch_shapes=[
            pltpu.VMEM((1, 16), F32),
            pltpu.VMEM((1, 12), F32),
            pltpu.VMEM((1, 256), F32),
            pltpu.VMEM((16, 64, 256), BF16),
            pltpu.VMEM((1024, 256), BF16),
            pltpu.VMEM((768, 256), BF16),
            pltpu.VMEM((1024, 768), F32),
            pltpu.VMEM((1024, 768), BF16),
            pltpu.VMEM((28, 32, 768), BF16),
            pltpu.VMEM((28, 32, 768), BF16),
            pltpu.VMEM((8, PIECES, 192, 128), BF16),
            pltpu.VMEM((2, 16, 256, 256), BF16),
            pltpu.SemaphoreType.DMA((N_SEND,)),
            pltpu.SemaphoreType.DMA((N_RECV,)),
            pltpu.SemaphoreType.DMA((6,)),
            pltpu.SemaphoreType.REGULAR,
            pltpu.SemaphoreType.REGULAR,
        ],
        compiler_params=pltpu.CompilerParams(
            collective_id=0, has_side_effects=True, vmem_limit_bytes=40 * 2**20
        ),
        cost_estimate=pl.CostEstimate(flops=2 * 1024 * 512 * 768 + 2 * 192 * 4096 * 256, bytes_accessed=2**21, transcendentals=0),
    )(
        *(
            pltpu.with_memory_space_constraint(operand, pltpu.HBM)
            for operand in (
                cholesky_a, cholesky_b.reshape(768, 256), amplitudes.reshape(256, 256),
                virtual_a.reshape(1, 16), virtual_b.reshape(1, 12), pair_energy.reshape(1, 256),
            )
        )
    )
    residual = other_terms + ladder.reshape(12, 16, 256).transpose(1, 0, 2)
    return (residual, residual / divisor.reshape(12, 16, 256).transpose(1, 0, 2))


def solution(mesh):
    return jax.shard_map(
        shards,
        mesh=mesh,
        in_specs=(
            P(("rep", "ab"), None, "ij"),
            P("rep", None, "ij"),
            P("ab", None, "ij"),
            P(("rep", "ab"), None, "ij"),
            P(("rep", "ab")),
            P("rep"),
            P("ij"),
        ),
        out_specs=(P(("rep", "ab"), None, "ij"), P(("rep", "ab"), None, "ij")),
        check_vma=False,
    )
```

```python
import jax
import jax.numpy as jnp
from jax import lax
from jax.experimental import pallas as pl
from jax.experimental.pallas import tpu as pltpu
from jax.sharding import PartitionSpec as P

MESH = pl.DeviceIdType.MESH
BF16, F32 = jnp.bfloat16, jnp.float32
RING = 8
PIECES = 4
LONG = {1: (0, 1), -1: (2, 3)}
SHORT = {1: (2, 3), -1: (0, 1)}
N_RECV, N_SEND = 49, 7


SLOTS = {
    key: i for i, key in enumerate(
        (s, stage, piece) for s in (1, -1) for stage in range(4) for piece in LONG[s] + (SHORT[s] if stage < 3 else ())
    )
}


def dot(a, b, dims):
    return lax.dot_general(a, b, (dims, ((), ())), preferred_element_type=F32)


def rotation(pieces, ways=(1, -1)):
    return [(s, pieces[s][i]) for i in range(PIECES // 2) for s in ways]


def kernel(a_hbm, b_hbm, t_hbm, va_hbm, vb_hbm, pe_hbm, out_ref, div_ref,
           va_ref, vb_ref, pe_ref, a_in, a_all, b_all, part, part_0, rs_in, rs_out, gath, t_all,
           send_sem, recv_sem, load_sem, go_sem, ready_sem):
    ab, ij, lo = lax.axis_index("ab"), lax.axis_index("ij"), lax.axis_index("rep")
    z, hi = ab // 2, ab % 2
    y, core = ij // 2, ij % 2
    sibling = (ab, y * 2 + 1 - core, lo)
    y_next = {s: (ab, ((y + s + RING) % RING) * 2 + core, lo) for s in (1, -1)}
    z_hop = {s: (((z + s + RING) % RING) * 2 + hi, ij, lo) for s in (1, -1)}
    x_far = (z * 2 + 1 - hi, ij, 1 - lo)
    x_near = (ab, ij, 1 - lo)
    x_far_sibling = (z * 2 + 1 - hi, y * 2 + 1 - core, 1 - lo)
    x_near_sibling = (ab, y * 2 + 1 - core, 1 - lo)

    numbers = ({}, {})

    def recv_of(to, name):
        if isinstance(name, tuple) and name[0] == "g":
            name = ("rs", *name[1:])
        return recv_sem.at[numbers[to].setdefault(name, len(numbers[to]))]

    def send(to, name, src, dst, device, group):
        pltpu.make_async_remote_copy(
            src_ref=src, dst_ref=dst, send_sem=send_sem.at[group], recv_sem=recv_of(to, name),
            device_id=device, device_id_type=MESH,
        ).start()

    def arrived(to, name, ref):
        pltpu.make_async_remote_copy(
            src_ref=ref, dst_ref=ref, send_sem=send_sem.at[0], recv_sem=recv_of(to, name),
            device_id=sibling, device_id_type=MESH,
        ).wait_recv()

    def sent(group, ref):
        pltpu.make_async_remote_copy(
            src_ref=ref, dst_ref=ref, send_sem=send_sem.at[group], recv_sem=recv_sem.at[0],
            device_id=sibling, device_id_type=MESH,
        ).wait_send()

    load_a = pltpu.make_async_copy(a_hbm, a_in, load_sem.at[0])
    load_b = pltpu.make_async_copy(b_hbm, b_all, load_sem.at[1])
    load_t = pltpu.make_async_copy(t_hbm, t_all.at[core, ab], load_sem.at[2])
    loads_small = [
        pltpu.make_async_copy(src, dst, load_sem.at[3 + i])
        for i, (src, dst) in enumerate(((va_hbm, va_ref), (vb_hbm, vb_ref), (pe_hbm, pe_ref)))
    ]

    barrier = pltpu.get_barrier_semaphore()

    def enter(friends):
        for friend in friends:
            pl.semaphore_signal(barrier, inc=1, device_id=friend, device_id_type=MESH)
        for load in (load_a, load_b, load_t, *loads_small):
            load.start()

    row = lax.broadcasted_iota(jnp.int32, (256, 256), 0)
    column = lax.broadcasted_iota(jnp.int32, (256, 256), 1)
    swap = jnp.where(column == (row % 16) * 16 + row // 16, 1.0, 0.0).astype(BF16)

    def reorder(k):
        block = ((y + 4) // 2 + k) % 4
        rows = a_in[:, pl.ds(pl.multiple_of(block * 16, 16), 16), :].reshape(256, 256)
        place = pl.ds(pl.multiple_of(block * 256, 256), 256)
        a_all[place, :] = dot(swap, rows, ((1,), (0,))).astype(BF16)

    def chunk_rows(offset):
        return pl.ds(pl.multiple_of(((y + offset + RING) % RING) * 128, 128), 128)

    def piece_rows(offset, piece):
        return pl.ds(pl.multiple_of(((y + offset + RING) % RING) * 128 + piece * 32, 32), 32)

    def products(ref, *offsets):
        left = jnp.concatenate([a_all[chunk_rows(offset), :] for offset in offsets], axis=0)
        value = dot(left, b_all[...], ((1,), (1,))).astype(ref.dtype)
        for i, offset in enumerate(offsets):
            ref[chunk_rows(offset), :] = value[i * 128:(i + 1) * 128]

    def divisor():
        for load in loads_small:
            load.wait()
        eye = lax.broadcasted_iota(jnp.int32, (16, 16), 0) == lax.broadcasted_iota(jnp.int32, (16, 16), 1)
        va = jnp.sum(jnp.where(eye, jnp.broadcast_to(va_ref[...], (16, 16)), 0.0), axis=1, keepdims=True)
        for b in range(12):
            div_ref[b * 16:(b + 1) * 16, :] = (va + vb_ref[0:1, b:b + 1]) - pe_ref[...]

    far_y = (y + 4) % RING
    ahead = (far_y - z + 2 + RING) % RING
    skipped = jnp.where(ahead < 5, ahead, 2)
    slabs_early = [(z - 2 + k + jnp.where(k >= skipped, 1, 0) + RING) % RING for k in range(4)]
    slabs_late = [(z + offset) % RING for offset in (3, 5, 4)]
    slabs_late = [jnp.where(slab == far_y, z, slab) for slab in slabs_late]

    def ladder(slabs):
        total = None
        for slab in slabs:
            left = jnp.concatenate([gath[slab, p] for p in range(PIECES)], axis=1)
            right = t_all[core, pl.ds(2 * slab, 2)].reshape(512, 256)
            product = dot(left, right, ((1,), (0,)))
            total = product if total is None else total + product
        return total

    def amplitudes(first_plane):
        friends = (*z_hop.values(), x_far, x_near)
        enter((sibling, *friends))

        def hand_products(*offsets):
            products(part_0, *offsets)
            if offsets == (4,):
                pl.semaphore_wait(go_sem, 1)
                for _, piece in rotation(LONG):
                    ref = part_0.at[piece_rows(4, piece)]
                    send(1, ("p", 4, piece), ref, ref, sibling, 0)
                return
            for offset in offsets:
                ref = part_0.at[chunk_rows(offset)]
                send(1, ("p", offsets[0]), ref, ref, sibling, 0)

        def own(offset):
            return ((z + offset + RING) % RING) * 2 + hi

        def other(offset):
            return ((z + offset + RING) % RING) * 2 + 1 - hi

        def half_rows(half):
            return pl.ds(half * 128, 128)

        def piece_of(slab, piece):
            return t_all.at[piece % 2, slab, half_rows(piece // 2)]

        def z_send(s, distance, piece):
            ref = piece_of(own(-s * (distance - 1)), piece)
            send(0, ("z", s, distance, piece), ref, ref, z_hop[s], 2)

        def far_send(offset, piece):
            ref = piece_of(own(offset), piece)

            def go():
                send(0, ("far", offset, piece // 2), ref, ref, x_far, 3)

            if offset != 4:
                pl.when(lo == 1 - piece % 2)(go)
            elif piece % 2:
                send(1, "t last", ref, ref, x_far_sibling, 3)
            else:
                go()

        def z_arrived(s, distance, piece):
            ref = piece_of(own(-s * distance), piece)
            arrived(0, ("z", s, distance, piece), ref)
            if distance < (4 if piece in LONG[s] else 3):
                z_send(s, distance + 1, piece)
            far_send(4 if distance == 4 else -s * distance, piece)
            if piece % 2:
                send(1, "t" if distance < 3 else "t last", ref, ref, sibling, 5)

        def near(offset, half):
            ref = t_all.at[lo, other(offset), half_rows(half)]
            arrived(0, ("far", offset, half), ref)
            late = " last" if abs(offset) == 3 else ""

            def column_0():
                send(0, "near" + late, ref, ref, x_near, 4)

            def column_1():
                send(1, "t" + late, ref, ref, x_near_sibling, 4)
                send(1, "t" + late, ref, ref, sibling, 6)

            pl.when(lo == 0)(column_0)
            pl.when(lo == 1)(column_1)

        def start_products():
            load_a.wait()
            reorder(0)
            load_b.wait()
            hand_products(4)
            for k in (1, 3, 2):
                reorder(k)

        def start_column(col):
            for pieces in (LONG, SHORT):
                for s in (1, -1):
                    z_send(s, 1, pieces[s][col])
            for half in range(2):
                far_send(0, 2 * half + col)

        def start_amplitudes():
            pl.semaphore_wait(barrier, len(friends))
            load_t.wait()
            start_column(0)

        def second_column():
            arrived(0, "t", t_all.at[1, ab])
            start_column(1)
            for friend in (x_near, x_far):
                pl.semaphore_signal(ready_sem, inc=1, device_id=friend, device_id_type=MESH)

        if first_plane:
            start_products()
            hand_products(3, -3)
            hand_products(2, -2)
            start_amplitudes()
            second_column()
        else:
            start_amplitudes()
            start_products()
            second_column()
            hand_products(3, -3)
            hand_products(2, -2)
        hand_products(1, -1)
        hand_products(0)
        divisor()

        for distance in (1, 2, 3, 4):
            for pieces in (LONG, SHORT) if distance < 4 else (LONG,):
                for s, piece in rotation(pieces):
                    z_arrived(s, distance, piece)
                if distance > 1:
                    for s in (1, -1):
                        near(-s * (distance - 1), pieces[s][0] // 2)
            if distance == 1:
                pl.semaphore_wait(ready_sem, 2)
                for half in range(2):
                    near(0, half)
        for s in (1, -1):
            near(-s * 3, SHORT[s][0] // 2)
        for half in range(2):
            arrived(0, ("far", 4, half), t_all.at[0, other(4), half_rows(half)])
        pl.when(lo == 1)(lambda: arrived(0, "near", t_all.at[0, 0:5]))
        arrived(0, "g early", gath.at[0:7])
        out_ref[...] = ladder(slabs_early)
        pl.when(lo == 1)(lambda: arrived(0, "near last", t_all.at[0, 0:2]))
        out_ref[...] += ladder(slabs_late)
        arrived(0, "g last", gath.at[0])
        out_ref[...] += ladder([far_y])

        sent(0, part_0)
        sent(2, t_all.at[0, 0:14])
        sent(3, t_all.at[0, 0:9])
        sent(4, t_all.at[0, 0:7])
        sent(5, t_all.at[0, 0:7])
        pl.when(lo == 1)(lambda: sent(6, t_all.at[0, 0:7]))

    def integrals(ways):
        enter(y_next.values())
        pl.semaphore_wait(barrier, 3)
        pl.semaphore_signal(go_sem, inc=1, device_id=sibling, device_id_type=MESH)
        send(0, "t", t_hbm, t_all.at[1, ab], sibling, 0)

        def own_part(offset, piece):
            rows = piece_rows(offset, piece)
            return part[rows, :] + part_0[rows, :].astype(F32)

        def received(s, stage, piece):
            slot = SLOTS[s, stage, piece]
            arrived(1, ("rs", s, stage, piece), rs_in.at[slot])
            return rs_in[slot].astype(F32)

        def rs_send(s, stage, piece):
            value = own_part(s * ((4 if piece in LONG[s] else 3) - stage), piece)
            if stage:
                value = value + received(s, stage - 1, piece)
            slot = SLOTS[s, stage, piece]
            rs_out[slot] = value.astype(BF16)
            send(1, ("rs", s, stage, piece), rs_out.at[slot], rs_in.at[slot], y_next[s], 1)

        def rs_stage(stage, pieces):
            for s, piece in rotation(pieces, ways):
                rs_send(s, stage, piece)

        load_a.wait()
        for k in range(4):
            reorder(k)
        load_b.wait()
        products(part, 4)
        products(part, 3, -3)
        products(part, 2, -2)
        for s, piece in rotation(LONG, ways):
            arrived(1, ("p", 4, piece), part_0.at[0:32])
            rs_send(s, 0, piece)
        arrived(1, ("p", 3), part_0.at[0:256])
        rs_stage(0, SHORT)
        products(part, 1, -1)
        products(part, 0)
        rs_stage(1, LONG)
        arrived(1, ("p", 2), part_0.at[0:256])
        rs_stage(1, SHORT)
        rs_stage(2, LONG)
        arrived(1, ("p", 1), part_0.at[0:256])
        rs_stage(2, SHORT)
        rs_stage(3, LONG)
        arrived(1, ("p", 0), part_0.at[0:128])

        def slab_of(offset):
            return (y + offset + RING) % RING

        def g_send(s, stage, piece):
            ref = gath.at[slab_of(-s * stage), piece]
            send(1, ("g", s, stage, piece), ref, ref, y_next[s], 2)

        def g_arrived(s, stage, piece):
            offset = -s * (stage + 1)
            arrived(1, ("g", s, stage, piece), gath.at[slab_of(offset), piece])
            if stage < (3 if piece in LONG[s] else 2):
                g_send(s, stage + 1, piece)
            g_hand(offset, piece)

        def g_hand(offset, piece):
            ref = gath.at[slab_of(offset), piece]
            send(0, "g last" if abs(offset) == 4 else "g early", ref, ref, sibling, 3)

        for way, piece in rotation(LONG, ways):
            value = own_part(0, piece)
            for s in (1, -1):
                value = value + received(s, 3 if piece in LONG[s] else 2, piece)
            for b in range(12):
                block = jnp.concatenate([value[c * 16:(c + 1) * 16, b * 64:(b + 1) * 64] for c in range(2)], axis=1)
                gath[y, piece, b * 16:(b + 1) * 16, :] = block.astype(BF16)
            g_send(way, 0, piece)
        for s, piece in rotation(SHORT, ways):
            g_send(s, 0, piece)
        for piece in range(PIECES):
            g_hand(0, piece)
        for stage in range(3):
            for pieces in (LONG, SHORT):
                for s, piece in rotation(pieces, ways):
                    g_arrived(s, stage, piece)
        divisor()
        load_t.wait()
        arrived(1, "t", t_all.at[1, 0:9])
        out_ref[...] = ladder(slabs_early)
        for s, piece in rotation(LONG, ways):
            g_arrived(s, 3, piece)
        arrived(1, "t last", t_all.at[1, 0:6])
        out_ref[...] += ladder([*slabs_late, far_y])

        sent(0, t_all.at[1, 0])
        sent(1, rs_out)
        sent(2, gath.at[0:7])
        sent(3, gath)

    pl.when((core == 1) & (y % 4 < 2))(lambda: integrals((-1, 1)))
    pl.when((core == 1) & (y % 4 >= 2))(lambda: integrals((1, -1)))
    pl.when((core == 0) & (z == 0))(lambda: amplitudes(True))
    pl.when((core == 0) & (z > 0))(lambda: amplitudes(False))
    assert max(map(len, numbers)) <= N_RECV


def shards(cholesky_a, cholesky_b, amplitudes, other_terms, virtual_a, virtual_b, pair_energy):
    hbm = pl.BlockSpec(memory_space=pltpu.HBM)
    vmem = pl.BlockSpec(memory_space=pltpu.VMEM)
    result = jax.ShapeDtypeStruct((192, 256), F32)
    ladder, divisor = pl.pallas_call(
        kernel,
        out_shape=(result, result),
        in_specs=[hbm] * 6,
        out_specs=(vmem, vmem),
        scratch_shapes=[
            pltpu.VMEM((1, 16), F32),
            pltpu.VMEM((1, 12), F32),
            pltpu.VMEM((1, 256), F32),
            pltpu.VMEM((16, 64, 256), BF16),
            pltpu.VMEM((1024, 256), BF16),
            pltpu.VMEM((768, 256), BF16),
            pltpu.VMEM((1024, 768), F32),
            pltpu.VMEM((1024, 768), BF16),
            pltpu.VMEM((28, 32, 768), BF16),
            pltpu.VMEM((28, 32, 768), BF16),
            pltpu.VMEM((8, PIECES, 192, 128), BF16),
            pltpu.VMEM((2, 16, 256, 256), BF16),
            pltpu.SemaphoreType.DMA((N_SEND,)),
            pltpu.SemaphoreType.DMA((N_RECV,)),
            pltpu.SemaphoreType.DMA((6,)),
            pltpu.SemaphoreType.REGULAR,
            pltpu.SemaphoreType.REGULAR,
        ],
        compiler_params=pltpu.CompilerParams(
            collective_id=0, has_side_effects=True, vmem_limit_bytes=40 * 2**20
        ),
        cost_estimate=pl.CostEstimate(flops=2 * 1024 * 512 * 768 + 2 * 192 * 4096 * 256, bytes_accessed=2**21, transcendentals=0),
    )(
        *(
            pltpu.with_memory_space_constraint(operand, pltpu.HBM)
            for operand in (
                cholesky_a, cholesky_b.reshape(768, 256), amplitudes.reshape(256, 256),
                virtual_a.reshape(1, 16), virtual_b.reshape(1, 12), pair_energy.reshape(1, 256),
            )
        )
    )
    residual = other_terms + ladder.reshape(12, 16, 256).transpose(1, 0, 2)
    return (residual, residual / divisor.reshape(12, 16, 256).transpose(1, 0, 2))


def solution(mesh):
    return jax.shard_map(
        shards,
        mesh=mesh,
        in_specs=(
            P(("rep", "ab"), None, "ij"),
            P("rep", None, "ij"),
            P("ab", None, "ij"),
            P(("rep", "ab"), None, "ij"),
            P(("rep", "ab")),
            P("rep"),
            P("ij"),
        ),
        out_specs=(P(("rep", "ab"), None, "ij"), P(("rep", "ab"), None, "ij")),
        check_vma=False,
    )
```

```python
import jax
import jax.numpy as jnp
from jax import lax
from jax.experimental import pallas as pl
from jax.experimental.pallas import tpu as pltpu
from jax.sharding import PartitionSpec as P

MESH = pl.DeviceIdType.MESH
BF16, F32 = jnp.bfloat16, jnp.float32
RING = 8
T_HOPS = {1: 3, -1: 4}
PIECES = 4
LONG = {1: (0, 1), -1: (2, 3)}
SHORT = {1: (2, 3), -1: (0, 1)}
N_RECV, N_SEND = 49, 7


SLOTS = {
    key: i for i, key in enumerate(
        (s, stage, piece) for s in (1, -1) for stage in range(4) for piece in LONG[s] + (SHORT[s] if stage < 3 else ())
    )
}


def dot(a, b, dims):
    return lax.dot_general(a, b, (dims, ((), ())), preferred_element_type=F32)


def rotation(pieces, ways=(1, -1)):
    return [(s, pieces[s][i]) for i in range(PIECES // 2) for s in ways]


def kernel(a_hbm, b_hbm, t_hbm, va_hbm, vb_hbm, pe_hbm, out_ref, div_ref,
           va_ref, vb_ref, pe_ref, a_in, a_all, b_all, part, part_0, rs_in, rs_out, gath, t_all,
           send_sem, recv_sem, load_sem, go_sem, ready_sem):
    ab, ij, lo = lax.axis_index("ab"), lax.axis_index("ij"), lax.axis_index("rep")
    z, hi = ab // 2, ab % 2
    y, core = ij // 2, ij % 2
    sibling = (ab, y * 2 + 1 - core, lo)
    y_next = {s: (ab, ((y + s + RING) % RING) * 2 + core, lo) for s in (1, -1)}
    z_hop = {s: (((z + s + RING) % RING) * 2 + hi, ij, lo) for s in (1, -1)}
    x_far = (z * 2 + 1 - hi, ij, 1 - lo)
    x_near = (ab, ij, 1 - lo)
    x_far_sibling = (z * 2 + 1 - hi, y * 2 + 1 - core, 1 - lo)
    x_near_sibling = (ab, y * 2 + 1 - core, 1 - lo)

    numbers = ({}, {})

    def recv_of(to, name):
        if isinstance(name, tuple) and name[0] == "g":
            name = ("rs", *name[1:])
        return recv_sem.at[numbers[to].setdefault(name, len(numbers[to]))]

    def send(to, name, src, dst, device, group):
        pltpu.make_async_remote_copy(
            src_ref=src, dst_ref=dst, send_sem=send_sem.at[group], recv_sem=recv_of(to, name),
            device_id=device, device_id_type=MESH,
        ).start()

    def arrived(to, name, ref):
        pltpu.make_async_remote_copy(
            src_ref=ref, dst_ref=ref, send_sem=send_sem.at[0], recv_sem=recv_of(to, name),
            device_id=sibling, device_id_type=MESH,
        ).wait_recv()

    def sent(group, ref):
        pltpu.make_async_remote_copy(
            src_ref=ref, dst_ref=ref, send_sem=send_sem.at[group], recv_sem=recv_sem.at[0],
            device_id=sibling, device_id_type=MESH,
        ).wait_send()

    load_a = pltpu.make_async_copy(a_hbm, a_in, load_sem.at[0])
    load_b = pltpu.make_async_copy(b_hbm, b_all, load_sem.at[1])
    load_t = pltpu.make_async_copy(t_hbm, t_all.at[core, ab], load_sem.at[2])
    loads_small = [
        pltpu.make_async_copy(src, dst, load_sem.at[3 + i])
        for i, (src, dst) in enumerate(((va_hbm, va_ref), (vb_hbm, vb_ref), (pe_hbm, pe_ref)))
    ]

    barrier = pltpu.get_barrier_semaphore()

    def enter(friends):
        for friend in friends:
            pl.semaphore_signal(barrier, inc=1, device_id=friend, device_id_type=MESH)
        for load in (load_a, load_b, load_t, *loads_small):
            load.start()

    row = lax.broadcasted_iota(jnp.int32, (256, 256), 0)
    column = lax.broadcasted_iota(jnp.int32, (256, 256), 1)
    swap = jnp.where(column == (row % 16) * 16 + row // 16, 1.0, 0.0).astype(BF16)

    def reorder(k):
        block = ((y + 4) // 2 + k) % 4
        rows = a_in[:, pl.ds(pl.multiple_of(block * 16, 16), 16), :].reshape(256, 256)
        place = pl.ds(pl.multiple_of(block * 256, 256), 256)
        a_all[place, :] = dot(swap, rows, ((1,), (0,))).astype(BF16)

    def chunk_rows(offset):
        return pl.ds(pl.multiple_of(((y + offset + RING) % RING) * 128, 128), 128)

    def piece_rows(offset, piece):
        return pl.ds(pl.multiple_of(((y + offset + RING) % RING) * 128 + piece * 32, 32), 32)

    def products(ref, *offsets):
        left = jnp.concatenate([a_all[chunk_rows(offset), :] for offset in offsets], axis=0)
        value = dot(left, b_all[...], ((1,), (1,))).astype(ref.dtype)
        for i, offset in enumerate(offsets):
            ref[chunk_rows(offset), :] = value[i * 128:(i + 1) * 128]

    def divisor():
        for load in loads_small:
            load.wait()
        eye = lax.broadcasted_iota(jnp.int32, (16, 16), 0) == lax.broadcasted_iota(jnp.int32, (16, 16), 1)
        va = jnp.sum(jnp.where(eye, jnp.broadcast_to(va_ref[...], (16, 16)), 0.0), axis=1, keepdims=True)
        for b in range(12):
            div_ref[b * 16:(b + 1) * 16, :] = (va + vb_ref[0:1, b:b + 1]) - pe_ref[...]

    far_y = (y + 4) % RING
    ahead = (far_y - z + 2 + RING) % RING
    skipped = jnp.where(ahead < 5, ahead, 2)
    slabs_early = [(z - 2 + k + jnp.where(k >= skipped, 1, 0) + RING) % RING for k in range(4)]
    slabs_late = [(z + offset) % RING for offset in (3, 5, 4)]
    slab_between = jnp.where(ahead < 5, far_y, z)
    slabs_late_y = [jnp.where(slab == far_y, z, slab) for slab in slabs_late]

    def ladder(slabs):
        total = None
        for slab in slabs:
            left = jnp.concatenate([gath[slab, p] for p in range(PIECES)], axis=1)
            right = t_all[core, pl.ds(2 * slab, 2)].reshape(512, 256)
            product = dot(left, right, ((1,), (0,)))
            total = product if total is None else total + product
        return total

    def amplitudes(first_plane):
        friends = (*z_hop.values(), x_far, x_near)
        enter((sibling, *friends))

        def hand_products(*offsets):
            products(part_0, *offsets)
            if offsets == (4,):
                pl.semaphore_wait(go_sem, 1)
                for _, piece in rotation(LONG):
                    ref = part_0.at[piece_rows(4, piece)]
                    send(1, ("p", 4, piece), ref, ref, sibling, 0)
                return
            for offset in offsets:
                ref = part_0.at[chunk_rows(offset)]
                send(1, ("p", offsets[0]), ref, ref, sibling, 0)

        def own(offset):
            return ((z + offset + RING) % RING) * 2 + hi

        def other(offset):
            return ((z + offset + RING) % RING) * 2 + 1 - hi

        def half_rows(half):
            return pl.ds(half * 128, 128)

        def piece_of(slab, piece):
            return t_all.at[piece % 2, slab, half_rows(piece // 2)]

        def z_send(s, distance, piece):
            ref = piece_of(own(-s * (distance - 1)), piece)
            send(0, ("z", s, distance, piece), ref, ref, z_hop[s], 2)

        def far_send(offset, piece):
            ref = piece_of(own(offset), piece)

            def go():
                send(0, ("far", offset, piece // 2), ref, ref, x_far, 3)

            if offset != 4:
                pl.when(lo == piece % 2)(go)
            elif piece % 2:
                send(1, "t last", ref, ref, x_far_sibling, 3)
            else:
                go()

        def z_arrived(s, distance, piece):
            ref = piece_of(own(-s * distance), piece)
            arrived(0, ("z", s, distance, piece), ref)
            if distance < T_HOPS[s]:
                z_send(s, distance + 1, piece)
            far_send(4 if distance == 4 else -s * distance, piece)
            if piece % 2:
                send(1, "t" if distance < 3 else "t last", ref, ref, sibling, 5)

        def near(offset, half):
            ref = t_all.at[1 - lo, other(offset), half_rows(half)]
            arrived(0, ("far", offset, half), ref)
            late = " last" if abs(offset) == 3 else ""

            def column_0():
                send(0, "near" + late, ref, ref, x_near, 4)

            def column_1():
                send(1, "t" + late, ref, ref, x_near_sibling, 4)
                send(1, "t" + late, ref, ref, sibling, 6)

            pl.when(lo == 1)(column_0)
            pl.when(lo == 0)(column_1)

        def start_products():
            load_a.wait()
            reorder(0)
            load_b.wait()
            hand_products(4)
            for k in (1, 3, 2):
                reorder(k)

        def start_column(col):
            for half in range(2):
                for s in (1, -1):
                    z_send(s, 1, 2 * half + col)
            for half in range(2):
                far_send(0, 2 * half + col)

        def start_amplitudes():
            pl.semaphore_wait(barrier, len(friends))
            load_t.wait()
            start_column(0)

        def second_column():
            arrived(0, "t", t_all.at[1, ab])
            start_column(1)
            for friend in (x_near, x_far):
                pl.semaphore_signal(ready_sem, inc=1, device_id=friend, device_id_type=MESH)

        if first_plane:
            start_products()
            hand_products(3, -3)
            hand_products(2, -2)
            start_amplitudes()
            second_column()
        else:
            start_amplitudes()
            start_products()
            second_column()
            hand_products(3, -3)
            hand_products(2, -2)
        hand_products(1, -1)
        hand_products(0)
        divisor()

        for distance in (1, 2, 3, 4):
            ways = (1, -1) if distance <= T_HOPS[1] else (-1,)
            for piece in (0, 2, 1, 3):
                if distance == 4 and piece == 3:
                    for s in (1, -1):
                        near(-s * 3, 0)
                for s in ways:
                    z_arrived(s, distance, piece)
            if distance > 1:
                for half in range(2) if distance < 4 else (1,):
                    for s in (1, -1):
                        near(-s * (distance - 1), half)
            if distance == 1:
                pl.semaphore_wait(ready_sem, 2)
                for half in range(2):
                    near(0, half)
        for half in range(2):
            arrived(0, ("far", 4, half), t_all.at[0, other(4), half_rows(half)])
        pl.when(lo == 0)(lambda: arrived(0, "near", t_all.at[0, 0:5]))
        arrived(0, "g early", gath.at[0:7])
        out_ref[...] = ladder(slabs_early)
        pl.when(lo == 0)(lambda: arrived(0, "near last", t_all.at[0, 0:2]))
        out_ref[...] += ladder(slabs_late_y)
        arrived(0, "g last", gath.at[0])
        out_ref[...] += ladder([far_y])

        sent(0, part_0)
        sent(2, t_all.at[0, 0:14])
        sent(3, t_all.at[0, 0:9])
        sent(4, t_all.at[0, 0:7])
        sent(5, t_all.at[0, 0:7])
        pl.when(lo == 0)(lambda: sent(6, t_all.at[0, 0:7]))

    def integrals(ways):
        enter(y_next.values())
        pl.semaphore_wait(barrier, 3)
        pl.semaphore_signal(go_sem, inc=1, device_id=sibling, device_id_type=MESH)
        send(0, "t", t_hbm, t_all.at[1, ab], sibling, 0)

        def own_part(offset, piece):
            rows = piece_rows(offset, piece)
            return part[rows, :] + part_0[rows, :].astype(F32)

        def received(s, stage, piece):
            slot = SLOTS[s, stage, piece]
            arrived(1, ("rs", s, stage, piece), rs_in.at[slot])
            return rs_in[slot].astype(F32)

        def rs_send(s, stage, piece):
            value = own_part(s * ((4 if piece in LONG[s] else 3) - stage), piece)
            if stage:
                value = value + received(s, stage - 1, piece)
            slot = SLOTS[s, stage, piece]
            rs_out[slot] = value.astype(BF16)
            send(1, ("rs", s, stage, piece), rs_out.at[slot], rs_in.at[slot], y_next[s], 1)

        def rs_stage(stage, pieces):
            for s, piece in rotation(pieces, ways):
                rs_send(s, stage, piece)

        load_a.wait()
        for k in range(4):
            reorder(k)
        load_b.wait()
        products(part, 4)
        products(part, 3, -3)
        products(part, 2, -2)
        for s, piece in rotation(LONG, ways):
            arrived(1, ("p", 4, piece), part_0.at[0:32])
            rs_send(s, 0, piece)
        arrived(1, ("p", 3), part_0.at[0:256])
        rs_stage(0, SHORT)
        products(part, 1, -1)
        products(part, 0)
        rs_stage(1, LONG)
        arrived(1, ("p", 2), part_0.at[0:256])
        rs_stage(1, SHORT)
        rs_stage(2, LONG)
        arrived(1, ("p", 1), part_0.at[0:256])
        rs_stage(2, SHORT)
        rs_stage(3, LONG)
        arrived(1, ("p", 0), part_0.at[0:128])

        def slab_of(offset):
            return (y + offset + RING) % RING

        def g_send(s, stage, piece):
            ref = gath.at[slab_of(-s * stage), piece]
            send(1, ("g", s, stage, piece), ref, ref, y_next[s], 2)

        def g_arrived(s, stage, piece):
            offset = -s * (stage + 1)
            arrived(1, ("g", s, stage, piece), gath.at[slab_of(offset), piece])
            if stage < (3 if piece in LONG[s] else 2):
                g_send(s, stage + 1, piece)
            g_hand(offset, piece)

        def g_hand(offset, piece):
            ref = gath.at[slab_of(offset), piece]
            send(0, "g last" if abs(offset) == 4 else "g early", ref, ref, sibling, 3)

        for way, piece in rotation(LONG, ways):
            value = own_part(0, piece)
            for s in (1, -1):
                value = value + received(s, 3 if piece in LONG[s] else 2, piece)
            for b in range(12):
                block = jnp.concatenate([value[c * 16:(c + 1) * 16, b * 64:(b + 1) * 64] for c in range(2)], axis=1)
                gath[y, piece, b * 16:(b + 1) * 16, :] = block.astype(BF16)
            g_send(way, 0, piece)
        for s, piece in rotation(SHORT, ways):
            g_send(s, 0, piece)
        for piece in range(PIECES):
            g_hand(0, piece)
        for stage in range(3):
            for pieces in (LONG, SHORT):
                for s, piece in rotation(pieces, ways):
                    g_arrived(s, stage, piece)
        divisor()
        load_t.wait()
        arrived(1, "t", t_all.at[1, 0:9])
        out_ref[...] = ladder(slabs_early)
        for s, piece in rotation(LONG, ways):
            g_arrived(s, 3, piece)
        out_ref[...] += ladder([slab_between])
        arrived(1, "t last", t_all.at[1, 0:6])
        out_ref[...] += ladder(slabs_late)

        sent(0, t_all.at[1, 0])
        sent(1, rs_out)
        sent(2, gath.at[0:7])
        sent(3, gath)

    pl.when((core == 1) & (y % 4 < 2))(lambda: integrals((-1, 1)))
    pl.when((core == 1) & (y % 4 >= 2))(lambda: integrals((1, -1)))
    pl.when((core == 0) & (z == 0))(lambda: amplitudes(True))
    pl.when((core == 0) & (z > 0))(lambda: amplitudes(False))
    assert max(map(len, numbers)) <= N_RECV


def shards(cholesky_a, cholesky_b, amplitudes, other_terms, virtual_a, virtual_b, pair_energy):
    hbm = pl.BlockSpec(memory_space=pltpu.HBM)
    vmem = pl.BlockSpec(memory_space=pltpu.VMEM)
    result = jax.ShapeDtypeStruct((192, 256), F32)
    ladder, divisor = pl.pallas_call(
        kernel,
        out_shape=(result, result),
        in_specs=[hbm] * 6,
        out_specs=(vmem, vmem),
        scratch_shapes=[
            pltpu.VMEM((1, 16), F32),
            pltpu.VMEM((1, 12), F32),
            pltpu.VMEM((1, 256), F32),
            pltpu.VMEM((16, 64, 256), BF16),
            pltpu.VMEM((1024, 256), BF16),
            pltpu.VMEM((768, 256), BF16),
            pltpu.VMEM((1024, 768), F32),
            pltpu.VMEM((1024, 768), BF16),
            pltpu.VMEM((28, 32, 768), BF16),
            pltpu.VMEM((28, 32, 768), BF16),
            pltpu.VMEM((8, PIECES, 192, 128), BF16),
            pltpu.VMEM((2, 16, 256, 256), BF16),
            pltpu.SemaphoreType.DMA((N_SEND,)),
            pltpu.SemaphoreType.DMA((N_RECV,)),
            pltpu.SemaphoreType.DMA((6,)),
            pltpu.SemaphoreType.REGULAR,
            pltpu.SemaphoreType.REGULAR,
        ],
        compiler_params=pltpu.CompilerParams(
            collective_id=0, has_side_effects=True, vmem_limit_bytes=40 * 2**20
        ),
        cost_estimate=pl.CostEstimate(flops=2 * 1024 * 512 * 768 + 2 * 192 * 4096 * 256, bytes_accessed=2**21, transcendentals=0),
    )(
        *(
            pltpu.with_memory_space_constraint(operand, pltpu.HBM)
            for operand in (
                cholesky_a, cholesky_b.reshape(768, 256), amplitudes.reshape(256, 256),
                virtual_a.reshape(1, 16), virtual_b.reshape(1, 12), pair_energy.reshape(1, 256),
            )
        )
    )
    residual = other_terms + ladder.reshape(12, 16, 256).transpose(1, 0, 2)
    return (residual, residual / divisor.reshape(12, 16, 256).transpose(1, 0, 2))


def solution(mesh):
    return jax.shard_map(
        shards,
        mesh=mesh,
        in_specs=(
            P(("rep", "ab"), None, "ij"),
            P("rep", None, "ij"),
            P("ab", None, "ij"),
            P(("rep", "ab"), None, "ij"),
            P(("rep", "ab")),
            P("rep"),
            P("ij"),
        ),
        out_specs=(P(("rep", "ab"), None, "ij"), P(("rep", "ab"), None, "ij")),
        check_vma=False,
    )
```

```python
import jax
import jax.numpy as jnp
from jax import lax
from jax.experimental import pallas as pl
from jax.experimental.pallas import tpu as pltpu
from jax.sharding import PartitionSpec as P

MESH = pl.DeviceIdType.MESH
BF16, F32 = jnp.bfloat16, jnp.float32
RING = 8
T_HOPS = {1: 3, -1: 4}
PIECES = 4
LONG = {1: (0, 1), -1: (2, 3)}
SHORT = {1: (2, 3), -1: (0, 1)}
N_RECV, N_SEND = 49, 7


SLOTS = {
    key: i for i, key in enumerate(
        (s, stage, piece) for s in (1, -1) for stage in range(4) for piece in LONG[s] + (SHORT[s] if stage < 3 else ())
    )
}


def dot(a, b, dims):
    return lax.dot_general(a, b, (dims, ((), ())), preferred_element_type=F32)


def rotation(pieces, ways=(1, -1)):
    return [(s, pieces[s][i]) for i in range(PIECES // 2) for s in ways]


def kernel(a_hbm, b_hbm, t_hbm, va_hbm, vb_hbm, pe_hbm, out_ref, div_ref,
           va_ref, vb_ref, pe_ref, a_in, a_all, b_all, part, part_0, rs_in, rs_out, gath, t_all,
           send_sem, recv_sem, load_sem, go_sem, ready_sem):
    ab, ij, lo = lax.axis_index("ab"), lax.axis_index("ij"), lax.axis_index("rep")
    z, hi = ab // 2, ab % 2
    y, core = ij // 2, ij % 2
    sibling = (ab, y * 2 + 1 - core, lo)
    y_next = {s: (ab, ((y + s + RING) % RING) * 2 + core, lo) for s in (1, -1)}
    z_hop = {s: (((z + s + RING) % RING) * 2 + hi, ij, lo) for s in (1, -1)}
    x_far = (z * 2 + 1 - hi, ij, 1 - lo)
    x_near = (ab, ij, 1 - lo)
    x_far_sibling = (z * 2 + 1 - hi, y * 2 + 1 - core, 1 - lo)
    x_near_sibling = (ab, y * 2 + 1 - core, 1 - lo)

    numbers = ({}, {})

    def recv_of(to, name):
        if isinstance(name, tuple) and name[0] == "g":
            name = ("rs", *name[1:])
        return recv_sem.at[numbers[to].setdefault(name, len(numbers[to]))]

    def send(to, name, src, dst, device, group):
        pltpu.make_async_remote_copy(
            src_ref=src, dst_ref=dst, send_sem=send_sem.at[group], recv_sem=recv_of(to, name),
            device_id=device, device_id_type=MESH,
        ).start()

    def arrived(to, name, ref):
        pltpu.make_async_remote_copy(
            src_ref=ref, dst_ref=ref, send_sem=send_sem.at[0], recv_sem=recv_of(to, name),
            device_id=sibling, device_id_type=MESH,
        ).wait_recv()

    def sent(group, ref):
        pltpu.make_async_remote_copy(
            src_ref=ref, dst_ref=ref, send_sem=send_sem.at[group], recv_sem=recv_sem.at[0],
            device_id=sibling, device_id_type=MESH,
        ).wait_send()

    load_a = pltpu.make_async_copy(a_hbm, a_in, load_sem.at[0])
    load_b = pltpu.make_async_copy(b_hbm, b_all, load_sem.at[1])
    load_t = pltpu.make_async_copy(t_hbm, t_all.at[core, ab], load_sem.at[2])
    loads_small = [
        pltpu.make_async_copy(src, dst, load_sem.at[3 + i])
        for i, (src, dst) in enumerate(((va_hbm, va_ref), (vb_hbm, vb_ref), (pe_hbm, pe_ref)))
    ]

    barrier = pltpu.get_barrier_semaphore()

    def enter(friends):
        for friend in friends:
            pl.semaphore_signal(barrier, inc=1, device_id=friend, device_id_type=MESH)
        for load in (load_a, load_b, load_t, *loads_small):
            load.start()

    def swap():
        row = lax.broadcasted_iota(jnp.int32, (256, 256), 0)
        column = lax.broadcasted_iota(jnp.int32, (256, 256), 1)
        return jnp.where(column == (row % 16) * 16 + row // 16, 1.0, 0.0).astype(BF16)

    def reorder(k, matrix):
        block = ((y + 4) // 2 + k) % 4
        rows = a_in[:, pl.ds(pl.multiple_of(block * 16, 16), 16), :].reshape(256, 256)
        place = pl.ds(pl.multiple_of(block * 256, 256), 256)
        a_all[place, :] = dot(matrix, rows, ((1,), (0,))).astype(BF16)

    def chunk_rows(offset):
        return pl.ds(pl.multiple_of(((y + offset + RING) % RING) * 128, 128), 128)

    def piece_rows(offset, piece):
        return pl.ds(pl.multiple_of(((y + offset + RING) % RING) * 128 + piece * 32, 32), 32)

    def products(ref, *offsets):
        left = jnp.concatenate([a_all[chunk_rows(offset), :] for offset in offsets], axis=0)
        value = dot(left, b_all[...], ((1,), (1,))).astype(ref.dtype)
        for i, offset in enumerate(offsets):
            ref[chunk_rows(offset), :] = value[i * 128:(i + 1) * 128]

    def divisor():
        for load in loads_small:
            load.wait()
        eye = lax.broadcasted_iota(jnp.int32, (16, 16), 0) == lax.broadcasted_iota(jnp.int32, (16, 16), 1)
        va = jnp.sum(jnp.where(eye, jnp.broadcast_to(va_ref[...], (16, 16)), 0.0), axis=1, keepdims=True)
        for b in range(12):
            div_ref[b * 16:(b + 1) * 16, :] = (va + vb_ref[0:1, b:b + 1]) - pe_ref[...]

    far_y = (y + 4) % RING
    ahead = (far_y - z + 2 + RING) % RING
    skipped = jnp.where(ahead < 5, ahead, 2)
    slabs_early = [(z - 2 + k + jnp.where(k >= skipped, 1, 0) + RING) % RING for k in range(4)]
    slabs_late = [(z + offset) % RING for offset in (3, 5, 4)]
    slab_between = jnp.where(ahead < 5, far_y, z)
    slabs_late_y = [jnp.where(slab == far_y, z, slab) for slab in slabs_late]

    def ladder(slabs):
        total = None
        for slab in slabs:
            left = jnp.concatenate([gath[slab, p] for p in range(PIECES)], axis=1)
            right = t_all[core, pl.ds(2 * slab, 2)].reshape(512, 256)
            product = dot(left, right, ((1,), (0,)))
            total = product if total is None else total + product
        return total

    def amplitudes(first_plane):
        friends = (*z_hop.values(), x_far, x_near)
        enter((sibling, *friends))

        def hand_products(*offsets):
            products(part_0, *offsets)
            if offsets == (4,):
                pl.semaphore_wait(go_sem, 1)
                for _, piece in rotation(LONG):
                    ref = part_0.at[piece_rows(4, piece)]
                    send(1, ("p", 4, piece), ref, ref, sibling, 0)
                return
            for offset in offsets:
                ref = part_0.at[chunk_rows(offset)]
                send(1, ("p", offsets[0]), ref, ref, sibling, 0)

        def own(offset):
            return ((z + offset + RING) % RING) * 2 + hi

        def other(offset):
            return ((z + offset + RING) % RING) * 2 + 1 - hi

        def half_rows(half):
            return pl.ds(half * 128, 128)

        def piece_of(slab, piece):
            return t_all.at[piece % 2, slab, half_rows(piece // 2)]

        def z_send(s, distance, piece):
            ref = piece_of(own(-s * (distance - 1)), piece)
            send(0, ("z", s, distance, piece), ref, ref, z_hop[s], 2)

        def far_send(offset, piece):
            ref = piece_of(own(offset), piece)

            def go():
                send(0, ("far", offset, piece // 2), ref, ref, x_far, 3)

            if offset != 4:
                pl.when(lo == piece % 2)(go)
            elif piece % 2:
                send(1, "t last", ref, ref, x_far_sibling, 3)
            else:
                go()

        def z_arrived(s, distance, piece):
            ref = piece_of(own(-s * distance), piece)
            arrived(0, ("z", s, distance, piece), ref)
            if distance < T_HOPS[s]:
                z_send(s, distance + 1, piece)
            far_send(4 if distance == 4 else -s * distance, piece)
            if piece % 2:
                send(1, "t" if distance < 3 else "t last", ref, ref, sibling, 5)

        def near(offset, half):
            ref = t_all.at[1 - lo, other(offset), half_rows(half)]
            arrived(0, ("far", offset, half), ref)
            late = " last" if abs(offset) == 3 else ""

            def column_0():
                send(0, "near" + late, ref, ref, x_near, 4)

            def column_1():
                send(1, "t" + late, ref, ref, x_near_sibling, 4)
                send(1, "t" + late, ref, ref, sibling, 6)

            pl.when(lo == 1)(column_0)
            pl.when(lo == 0)(column_1)

        def start_products():
            matrix = swap()
            load_a.wait()
            reorder(0, matrix)
            load_b.wait()
            hand_products(4)
            for k in (1, 3, 2):
                reorder(k, matrix)

        def start_column(col):
            for half in range(2):
                for s in (1, -1):
                    z_send(s, 1, 2 * half + col)
            for half in range(2):
                far_send(0, 2 * half + col)

        def start_amplitudes():
            pl.semaphore_wait(barrier, len(friends))
            load_t.wait()
            start_column(0)

        def second_column():
            arrived(0, "t", t_all.at[1, ab])
            start_column(1)
            for friend in (x_near, x_far):
                pl.semaphore_signal(ready_sem, inc=1, device_id=friend, device_id_type=MESH)

        if first_plane:
            start_products()
            hand_products(3, -3)
            hand_products(2, -2)
            start_amplitudes()
            second_column()
        else:
            start_amplitudes()
            start_products()
            second_column()
            hand_products(3, -3)
            hand_products(2, -2)
        hand_products(1, -1)
        hand_products(0)
        divisor()

        turns = (0, 2, 1, 3)

        def both(distance):
            for piece in turns:
                for s in (1, -1):
                    z_arrived(s, distance, piece)

        def near_both(distance, half):
            for s in (1, -1):
                near(-s * distance, half)

        both(1)
        pl.semaphore_wait(ready_sem, 2)
        for half in range(2):
            near(0, half)
        for distance in (2, 3):
            both(distance)
            for half in range(2):
                near_both(distance - 1, half)
        for piece in (0, 1):
            z_arrived(-1, 4, piece)
        near_both(3, 0)
        for piece in (3, 2):
            z_arrived(-1, 4, piece)
        near_both(3, 1)
        for half in range(2):
            arrived(0, ("far", 4, half), t_all.at[0, other(4), half_rows(half)])
        pl.when(lo == 0)(lambda: arrived(0, "near", t_all.at[0, 0:5]))
        arrived(0, "g early", gath.at[0:7])
        out_ref[...] = ladder(slabs_early)
        pl.when(lo == 0)(lambda: arrived(0, "near last", t_all.at[0, 0:2]))
        out_ref[...] += ladder(slabs_late_y)
        arrived(0, "g last", gath.at[0])
        out_ref[...] += ladder([far_y])

        sent(0, part_0)
        sent(2, t_all.at[0, 0:14])
        sent(3, t_all.at[0, 0:9])
        sent(4, t_all.at[0, 0:7])
        sent(5, t_all.at[0, 0:7])
        pl.when(lo == 0)(lambda: sent(6, t_all.at[0, 0:7]))

    def integrals(ways):
        enter(y_next.values())
        pl.semaphore_wait(barrier, 3)
        pl.semaphore_signal(go_sem, inc=1, device_id=sibling, device_id_type=MESH)
        send(0, "t", t_hbm, t_all.at[1, ab], sibling, 0)

        def own_part(offset, piece):
            rows = piece_rows(offset, piece)
            return part[rows, :] + part_0[rows, :].astype(F32)

        def received(s, stage, piece):
            slot = SLOTS[s, stage, piece]
            arrived(1, ("rs", s, stage, piece), rs_in.at[slot])
            return rs_in[slot].astype(F32)

        def rs_send(s, stage, piece):
            value = own_part(s * ((4 if piece in LONG[s] else 3) - stage), piece)
            if stage:
                value = value + received(s, stage - 1, piece)
            slot = SLOTS[s, stage, piece]
            rs_out[slot] = value.astype(BF16)
            send(1, ("rs", s, stage, piece), rs_out.at[slot], rs_in.at[slot], y_next[s], 1)

        def rs_stage(stage, pieces):
            for s, piece in rotation(pieces, ways):
                rs_send(s, stage, piece)

        matrix = swap()
        load_a.wait()
        for k in range(4):
            reorder(k, matrix)
        load_b.wait()
        products(part, 4)
        products(part, 3, -3)
        products(part, 2, -2)
        for s, piece in rotation(LONG, ways):
            arrived(1, ("p", 4, piece), part_0.at[0:32])
            rs_send(s, 0, piece)
        arrived(1, ("p", 3), part_0.at[0:256])
        rs_stage(0, SHORT)
        products(part, 1, -1)
        products(part, 0)
        rs_stage(1, LONG)
        arrived(1, ("p", 2), part_0.at[0:256])
        rs_stage(1, SHORT)
        rs_stage(2, LONG)
        arrived(1, ("p", 1), part_0.at[0:256])
        rs_stage(2, SHORT)
        rs_stage(3, LONG)
        arrived(1, ("p", 0), part_0.at[0:128])

        def slab_of(offset):
            return (y + offset + RING) % RING

        def g_send(s, stage, piece):
            ref = gath.at[slab_of(-s * stage), piece]
            send(1, ("g", s, stage, piece), ref, ref, y_next[s], 2)

        def g_arrived(s, stage, piece):
            offset = -s * (stage + 1)
            arrived(1, ("g", s, stage, piece), gath.at[slab_of(offset), piece])
            if stage < (3 if piece in LONG[s] else 2):
                g_send(s, stage + 1, piece)
            g_hand(offset, piece)

        def g_hand(offset, piece):
            ref = gath.at[slab_of(offset), piece]
            send(0, "g last" if abs(offset) == 4 else "g early", ref, ref, sibling, 3)

        for way, piece in rotation(LONG, ways):
            value = own_part(0, piece)
            for s in (1, -1):
                value = value + received(s, 3 if piece in LONG[s] else 2, piece)
            for b in range(12):
                block = jnp.concatenate([value[c * 16:(c + 1) * 16, b * 64:(b + 1) * 64] for c in range(2)], axis=1)
                gath[y, piece, b * 16:(b + 1) * 16, :] = block.astype(BF16)
            g_send(way, 0, piece)
        for s, piece in rotation(SHORT, ways):
            g_send(s, 0, piece)
        for piece in range(PIECES):
            g_hand(0, piece)
        for stage in range(3):
            for pieces in (LONG, SHORT):
                for s, piece in rotation(pieces, ways):
                    g_arrived(s, stage, piece)
        divisor()
        load_t.wait()
        arrived(1, "t", t_all.at[1, 0:9])
        out_ref[...] = ladder(slabs_early)
        for s, piece in rotation(LONG, ways):
            g_arrived(s, 3, piece)
        out_ref[...] += ladder([slab_between])
        arrived(1, "t last", t_all.at[1, 0:6])
        out_ref[...] += ladder(slabs_late)

        sent(0, t_all.at[1, 0])
        sent(1, rs_out)
        sent(2, gath.at[0:7])
        sent(3, gath)

    pl.when((core == 1) & (y % 4 < 2))(lambda: integrals((-1, 1)))
    pl.when((core == 1) & (y % 4 >= 2))(lambda: integrals((1, -1)))
    pl.when((core == 0) & (z == 0))(lambda: amplitudes(True))
    pl.when((core == 0) & (z > 0))(lambda: amplitudes(False))
    assert max(map(len, numbers)) <= N_RECV


def shards(cholesky_a, cholesky_b, amplitudes, other_terms, virtual_a, virtual_b, pair_energy):
    hbm = pl.BlockSpec(memory_space=pltpu.HBM)
    vmem = pl.BlockSpec(memory_space=pltpu.VMEM)
    result = jax.ShapeDtypeStruct((192, 256), F32)
    ladder, divisor = pl.pallas_call(
        kernel,
        out_shape=(result, result),
        in_specs=[hbm] * 6,
        out_specs=(vmem, vmem),
        scratch_shapes=[
            pltpu.VMEM((1, 16), F32),
            pltpu.VMEM((1, 12), F32),
            pltpu.VMEM((1, 256), F32),
            pltpu.VMEM((16, 64, 256), BF16),
            pltpu.VMEM((1024, 256), BF16),
            pltpu.VMEM((768, 256), BF16),
            pltpu.VMEM((1024, 768), F32),
            pltpu.VMEM((1024, 768), BF16),
            pltpu.VMEM((28, 32, 768), BF16),
            pltpu.VMEM((28, 32, 768), BF16),
            pltpu.VMEM((8, PIECES, 192, 128), BF16),
            pltpu.VMEM((2, 16, 256, 256), BF16),
            pltpu.SemaphoreType.DMA((N_SEND,)),
            pltpu.SemaphoreType.DMA((N_RECV,)),
            pltpu.SemaphoreType.DMA((6,)),
            pltpu.SemaphoreType.REGULAR,
            pltpu.SemaphoreType.REGULAR,
        ],
        compiler_params=pltpu.CompilerParams(
            collective_id=0, has_side_effects=True, vmem_limit_bytes=40 * 2**20
        ),
        cost_estimate=pl.CostEstimate(flops=2 * 1024 * 512 * 768 + 2 * 192 * 4096 * 256, bytes_accessed=2**21, transcendentals=0),
    )(
        *(
            pltpu.with_memory_space_constraint(operand, pltpu.HBM)
            for operand in (
                cholesky_a, cholesky_b.reshape(768, 256), amplitudes.reshape(256, 256),
                virtual_a.reshape(1, 16), virtual_b.reshape(1, 12), pair_energy.reshape(1, 256),
            )
        )
    )
    residual = other_terms + ladder.reshape(12, 16, 256).transpose(1, 0, 2)
    return (residual, residual / divisor.reshape(12, 16, 256).transpose(1, 0, 2))


def solution(mesh):
    return jax.shard_map(
        shards,
        mesh=mesh,
        in_specs=(
            P(("rep", "ab"), None, "ij"),
            P("rep", None, "ij"),
            P("ab", None, "ij"),
            P(("rep", "ab"), None, "ij"),
            P(("rep", "ab")),
            P("rep"),
            P("ij"),
        ),
        out_specs=(P(("rep", "ab"), None, "ij"), P(("rep", "ab"), None, "ij")),
        check_vma=False,
    )
```

```python
import jax
import jax.numpy as jnp
from jax import lax
from jax.experimental import pallas as pl
from jax.experimental.pallas import tpu as pltpu
from jax.sharding import PartitionSpec as P

MESH = pl.DeviceIdType.MESH
BF16, F32 = jnp.bfloat16, jnp.float32
RING = 8
T_HOPS = {1: 3, -1: 4}
PIECES = 4
LONG = {1: (0, 1), -1: (2, 3)}
SHORT = {1: (2, 3), -1: (0, 1)}
N_RECV, N_SEND = 49, 7


SLOTS = {
    key: i for i, key in enumerate(
        (s, stage, piece) for s in (1, -1) for stage in range(4) for piece in LONG[s] + (SHORT[s] if stage < 3 else ())
    )
}


def dot(a, b, dims):
    return lax.dot_general(a, b, (dims, ((), ())), preferred_element_type=F32)


def rotation(pieces, ways=(1, -1)):
    return [(s, pieces[s][i]) for i in range(PIECES // 2) for s in ways]


def kernel(a_hbm, b_hbm, t_hbm, va_hbm, vb_hbm, pe_hbm, out_ref, div_ref,
           va_ref, vb_ref, pe_ref, a_in, a_all, b_all, part, part_0, rs_in, rs_out, gath, t_all,
           send_sem, recv_sem, load_sem, go_sem, ready_sem):
    ab, ij, lo = lax.axis_index("ab"), lax.axis_index("ij"), lax.axis_index("rep")
    z, hi = ab // 2, ab % 2
    y, core = ij // 2, ij % 2
    sibling = (ab, y * 2 + 1 - core, lo)
    y_next = {s: (ab, ((y + s + RING) % RING) * 2 + core, lo) for s in (1, -1)}
    z_hop = {s: (((z + s + RING) % RING) * 2 + hi, ij, lo) for s in (1, -1)}
    x_far = (z * 2 + 1 - hi, ij, 1 - lo)
    x_near = (ab, ij, 1 - lo)
    x_far_sibling = (z * 2 + 1 - hi, y * 2 + 1 - core, 1 - lo)
    x_near_sibling = (ab, y * 2 + 1 - core, 1 - lo)

    numbers = ({}, {})

    def recv_of(to, name):
        if isinstance(name, tuple) and name[0] == "g":
            name = ("rs", *name[1:])
        return recv_sem.at[numbers[to].setdefault(name, len(numbers[to]))]

    def send(to, name, src, dst, device, group):
        pltpu.make_async_remote_copy(
            src_ref=src, dst_ref=dst, send_sem=send_sem.at[group], recv_sem=recv_of(to, name),
            device_id=device, device_id_type=MESH,
        ).start()

    def arrived(to, name, ref):
        pltpu.make_async_remote_copy(
            src_ref=ref, dst_ref=ref, send_sem=send_sem.at[0], recv_sem=recv_of(to, name),
            device_id=sibling, device_id_type=MESH,
        ).wait_recv()

    def sent(group, ref):
        pltpu.make_async_remote_copy(
            src_ref=ref, dst_ref=ref, send_sem=send_sem.at[group], recv_sem=recv_sem.at[0],
            device_id=sibling, device_id_type=MESH,
        ).wait_send()

    load_a = pltpu.make_async_copy(a_hbm, a_in, load_sem.at[0])
    load_b = pltpu.make_async_copy(b_hbm, b_all, load_sem.at[1])
    load_t = pltpu.make_async_copy(t_hbm, t_all.at[core, ab], load_sem.at[2])
    loads_small = [
        pltpu.make_async_copy(src, dst, load_sem.at[3 + i])
        for i, (src, dst) in enumerate(((va_hbm, va_ref), (vb_hbm, vb_ref), (pe_hbm, pe_ref)))
    ]

    barrier = pltpu.get_barrier_semaphore()

    def enter(friends):
        for friend in friends:
            pl.semaphore_signal(barrier, inc=1, device_id=friend, device_id_type=MESH)
        for load in (load_a, load_b, load_t, *loads_small):
            load.start()

    def swap():
        row = lax.broadcasted_iota(jnp.int32, (256, 256), 0)
        column = lax.broadcasted_iota(jnp.int32, (256, 256), 1)
        return jnp.where(column == (row % 16) * 16 + row // 16, 1.0, 0.0).astype(BF16)

    def reorder(k, matrix):
        block = ((y + 4) // 2 + k) % 4
        rows = a_in[:, pl.ds(pl.multiple_of(block * 16, 16), 16), :].reshape(256, 256)
        place = pl.ds(pl.multiple_of(block * 256, 256), 256)
        a_all[place, :] = dot(matrix, rows, ((1,), (0,))).astype(BF16)

    def chunk_rows(offset):
        return pl.ds(pl.multiple_of(((y + offset + RING) % RING) * 128, 128), 128)

    def piece_rows(offset, piece):
        return pl.ds(pl.multiple_of(((y + offset + RING) % RING) * 128 + piece * 32, 32), 32)

    def products(ref, *offsets):
        left = jnp.concatenate([a_all[chunk_rows(offset), :] for offset in offsets], axis=0)
        value = dot(left, b_all[...], ((1,), (1,))).astype(ref.dtype)
        for i, offset in enumerate(offsets):
            ref[chunk_rows(offset), :] = value[i * 128:(i + 1) * 128]

    def divisor():
        for load in loads_small:
            load.wait()
        eye = lax.broadcasted_iota(jnp.int32, (16, 16), 0) == lax.broadcasted_iota(jnp.int32, (16, 16), 1)
        va = jnp.sum(jnp.where(eye, jnp.broadcast_to(va_ref[...], (16, 16)), 0.0), axis=1, keepdims=True)
        for b in range(12):
            div_ref[b * 16:(b + 1) * 16, :] = (va + vb_ref[0:1, b:b + 1]) - pe_ref[...]

    far_y = (y + 4) % RING
    ahead = (far_y - z + 2 + RING) % RING
    skipped = jnp.where(ahead < 5, ahead, 2)
    slabs_early = [(z - 2 + k + jnp.where(k >= skipped, 1, 0) + RING) % RING for k in range(4)]
    slabs_late = [(z + offset) % RING for offset in (3, 5, 4)]
    slab_between = jnp.where(ahead < 5, far_y, z)

    def ladder_of(slabs, half):
        left = [gath[slab, 2 * half + p] for slab in slabs for p in range(PIECES // 2)]
        right = [t_all[core, 2 * slab + half] for slab in slabs]
        return dot(jnp.concatenate(left, axis=1), jnp.concatenate(right, axis=0), ((1,), (0,)))

    def ladder(slabs):
        total = None
        for slab in slabs:
            left = jnp.concatenate([gath[slab, p] for p in range(PIECES)], axis=1)
            right = t_all[core, pl.ds(2 * slab, 2)].reshape(512, 256)
            product = dot(left, right, ((1,), (0,)))
            total = product if total is None else total + product
        return total

    def amplitudes(first_plane):
        friends = (*z_hop.values(), x_far, x_near)
        enter((sibling, *friends))

        def hand_products(*offsets):
            products(part_0, *offsets)
            if offsets == (4,):
                pl.semaphore_wait(go_sem, 1)
                for _, piece in rotation(LONG):
                    ref = part_0.at[piece_rows(4, piece)]
                    send(1, ("p", 4, piece), ref, ref, sibling, 0)
                return
            for offset in offsets:
                ref = part_0.at[chunk_rows(offset)]
                send(1, ("p", offsets[0]), ref, ref, sibling, 0)

        def own(offset):
            return ((z + offset + RING) % RING) * 2 + hi

        def other(offset):
            return ((z + offset + RING) % RING) * 2 + 1 - hi

        def half_rows(half):
            return pl.ds(half * 128, 128)

        def piece_of(slab, piece):
            return t_all.at[piece % 2, slab, half_rows(piece // 2)]

        def z_send(s, distance, piece):
            ref = piece_of(own(-s * (distance - 1)), piece)
            send(0, ("z", s, distance, piece), ref, ref, z_hop[s], 2)

        def far_send(offset, piece):
            ref = piece_of(own(offset), piece)

            def go():
                send(0, ("far", offset, piece // 2), ref, ref, x_far, 3)

            if offset != 4:
                pl.when(lo == piece % 2)(go)
            elif piece % 2:
                send(1, "t last", ref, ref, x_far_sibling, 3)
            else:
                go()

        def z_arrived(s, distance, piece):
            ref = piece_of(own(-s * distance), piece)
            arrived(0, ("z", s, distance, piece), ref)
            if distance < T_HOPS[s]:
                z_send(s, distance + 1, piece)
            far_send(4 if distance == 4 else -s * distance, piece)
            if piece % 2:
                send(1, "t" if distance < 3 else "t own", ref, ref, sibling, 5)

        def near(offset, half):
            ref = t_all.at[1 - lo, other(offset), half_rows(half)]
            arrived(0, ("far", offset, half), ref)
            late = " last" if abs(offset) == 3 else ""

            def column_0():
                send(0, "near" + late, ref, ref, x_near, 4)

            def column_1():
                send(1, "t" + late, ref, ref, x_near_sibling, 4)
                send(1, "t" + late, ref, ref, sibling, 6)

            pl.when(lo == 1)(column_0)
            pl.when(lo == 0)(column_1)

        def more_products():
            for k in (1, 3, 2):
                reorder(k, matrix)
            hand_products(3, -3)
            hand_products(2, -2)

        def start_column(col):
            for half in range(2):
                for s in (1, -1):
                    z_send(s, 1, 2 * half + col)
            for half in range(2):
                far_send(0, 2 * half + col)

        def start_amplitudes():
            pl.semaphore_wait(barrier, len(friends))
            load_t.wait()
            start_column(0)

        def second_column():
            arrived(0, "t", t_all.at[1, ab])
            start_column(1)
            for friend in (x_near, x_far):
                pl.semaphore_signal(ready_sem, inc=1, device_id=friend, device_id_type=MESH)

        matrix = swap()
        if not first_plane:
            start_amplitudes()
        load_a.wait()
        reorder(0, matrix)
        load_b.wait()
        hand_products(4)
        if first_plane:
            more_products()
            start_amplitudes()
        second_column()
        if not first_plane:
            more_products()
        hand_products(1, -1)
        hand_products(0)
        divisor()

        turns = (0, 2, 1, 3)

        def both(distance):
            for piece in turns:
                for s in (1, -1):
                    z_arrived(s, distance, piece)

        def near_both(distance, half):
            for s in (1, -1):
                near(-s * distance, half)

        both(1)
        pl.semaphore_wait(ready_sem, 2)
        for half in range(2):
            near(0, half)
        for distance in (2, 3):
            both(distance)
            for half in range(2):
                near_both(distance - 1, half)
        for piece in (0, 1):
            z_arrived(-1, 4, piece)
        near_both(3, 0)
        for piece in (3, 2):
            z_arrived(-1, 4, piece)
        near_both(3, 1)
        pl.when(lo == 0)(lambda: arrived(0, "near", t_all.at[0, 0:5]))
        arrived(0, "g early", gath.at[0:7])
        out_ref[...] = ladder(slabs_early)
        arrived(0, "g last", gath.at[0])
        out_ref[...] += ladder([slab_between]) + ladder_of(slabs_late, hi)
        for half in range(2):
            arrived(0, ("far", 4, half), t_all.at[0, other(4), half_rows(half)])
        pl.when(lo == 0)(lambda: arrived(0, "near last", t_all.at[0, 0:2]))
        out_ref[...] += ladder_of(slabs_late, 1 - hi)

        sent(0, part_0)
        sent(2, t_all.at[0, 0:14])
        sent(3, t_all.at[0, 0:9])
        sent(4, t_all.at[0, 0:7])
        sent(5, t_all.at[0, 0:7])
        pl.when(lo == 0)(lambda: sent(6, t_all.at[0, 0:7]))

    def integrals(ways):
        enter(y_next.values())
        pl.semaphore_wait(barrier, 3)
        pl.semaphore_signal(go_sem, inc=1, device_id=sibling, device_id_type=MESH)
        send(0, "t", t_hbm, t_all.at[1, ab], sibling, 0)

        def own_part(offset, piece):
            rows = piece_rows(offset, piece)
            return part[rows, :] + part_0[rows, :].astype(F32)

        def received(s, stage, piece):
            slot = SLOTS[s, stage, piece]
            arrived(1, ("rs", s, stage, piece), rs_in.at[slot])
            return rs_in[slot].astype(F32)

        def rs_send(s, stage, piece):
            value = own_part(s * ((4 if piece in LONG[s] else 3) - stage), piece)
            if stage:
                value = value + received(s, stage - 1, piece)
            slot = SLOTS[s, stage, piece]
            rs_out[slot] = value.astype(BF16)
            send(1, ("rs", s, stage, piece), rs_out.at[slot], rs_in.at[slot], y_next[s], 1)

        def rs_stage(stage, pieces):
            for s, piece in rotation(pieces, ways):
                rs_send(s, stage, piece)

        matrix = swap()
        load_a.wait()
        for k in range(4):
            reorder(k, matrix)
        load_b.wait()
        products(part, 4)
        products(part, 3, -3)
        products(part, 2, -2)
        for s, piece in rotation(LONG, ways):
            arrived(1, ("p", 4, piece), part_0.at[0:32])
            rs_send(s, 0, piece)
        arrived(1, ("p", 3), part_0.at[0:256])
        rs_stage(0, SHORT)
        products(part, 1, -1)
        products(part, 0)
        rs_stage(1, LONG)
        arrived(1, ("p", 2), part_0.at[0:256])
        rs_stage(1, SHORT)
        rs_stage(2, LONG)
        arrived(1, ("p", 1), part_0.at[0:256])
        rs_stage(2, SHORT)
        rs_stage(3, LONG)
        arrived(1, ("p", 0), part_0.at[0:128])

        def slab_of(offset):
            return (y + offset + RING) % RING

        def g_send(s, stage, piece):
            ref = gath.at[slab_of(-s * stage), piece]
            send(1, ("g", s, stage, piece), ref, ref, y_next[s], 2)

        def g_arrived(s, stage, piece):
            offset = -s * (stage + 1)
            arrived(1, ("g", s, stage, piece), gath.at[slab_of(offset), piece])
            if stage < (3 if piece in LONG[s] else 2):
                g_send(s, stage + 1, piece)
            g_hand(offset, piece)

        def g_hand(offset, piece):
            ref = gath.at[slab_of(offset), piece]
            send(0, "g last" if abs(offset) == 4 else "g early", ref, ref, sibling, 3)

        for way, piece in rotation(LONG, ways):
            value = own_part(0, piece)
            for s in (1, -1):
                value = value + received(s, 3 if piece in LONG[s] else 2, piece)
            for b in range(12):
                block = jnp.concatenate([value[c * 16:(c + 1) * 16, b * 64:(b + 1) * 64] for c in range(2)], axis=1)
                gath[y, piece, b * 16:(b + 1) * 16, :] = block.astype(BF16)
            g_send(way, 0, piece)
        for s, piece in rotation(SHORT, ways):
            g_send(s, 0, piece)
        for piece in range(PIECES):
            g_hand(0, piece)
        for stage in range(3):
            for pieces in (LONG, SHORT):
                for s, piece in rotation(pieces, ways):
                    g_arrived(s, stage, piece)
        divisor()
        load_t.wait()
        arrived(1, "t", t_all.at[1, 0:9])
        out_ref[...] = ladder(slabs_early)
        for s, piece in rotation(LONG, ways):
            g_arrived(s, 3, piece)
        arrived(1, "t own", t_all.at[1, 0:3])
        out_ref[...] += ladder([slab_between]) + ladder_of(slabs_late, hi)
        arrived(1, "t last", t_all.at[1, 0:3])
        out_ref[...] += ladder_of(slabs_late, 1 - hi)

        sent(0, t_all.at[1, 0])
        sent(1, rs_out)
        sent(2, gath.at[0:7])
        sent(3, gath)

    pl.when((core == 1) & (y % 4 < 2))(lambda: integrals((-1, 1)))
    pl.when((core == 1) & (y % 4 >= 2))(lambda: integrals((1, -1)))
    pl.when((core == 0) & (z == 0))(lambda: amplitudes(True))
    pl.when((core == 0) & (z > 0))(lambda: amplitudes(False))
    assert max(map(len, numbers)) <= N_RECV


def shards(cholesky_a, cholesky_b, amplitudes, other_terms, virtual_a, virtual_b, pair_energy):
    hbm = pl.BlockSpec(memory_space=pltpu.HBM)
    vmem = pl.BlockSpec(memory_space=pltpu.VMEM)
    result = jax.ShapeDtypeStruct((192, 256), F32)
    ladder, divisor = pl.pallas_call(
        kernel,
        out_shape=(result, result),
        in_specs=[hbm] * 6,
        out_specs=(vmem, vmem),
        scratch_shapes=[
            pltpu.VMEM((1, 16), F32),
            pltpu.VMEM((1, 12), F32),
            pltpu.VMEM((1, 256), F32),
            pltpu.VMEM((16, 64, 256), BF16),
            pltpu.VMEM((1024, 256), BF16),
            pltpu.VMEM((768, 256), BF16),
            pltpu.VMEM((1024, 768), F32),
            pltpu.VMEM((1024, 768), BF16),
            pltpu.VMEM((28, 32, 768), BF16),
            pltpu.VMEM((28, 32, 768), BF16),
            pltpu.VMEM((8, PIECES, 192, 128), BF16),
            pltpu.VMEM((2, 16, 256, 256), BF16),
            pltpu.SemaphoreType.DMA((N_SEND,)),
            pltpu.SemaphoreType.DMA((N_RECV,)),
            pltpu.SemaphoreType.DMA((6,)),
            pltpu.SemaphoreType.REGULAR,
            pltpu.SemaphoreType.REGULAR,
        ],
        compiler_params=pltpu.CompilerParams(
            collective_id=0, has_side_effects=True, vmem_limit_bytes=40 * 2**20
        ),
        cost_estimate=pl.CostEstimate(flops=2 * 1024 * 512 * 768 + 2 * 192 * 4096 * 256, bytes_accessed=2**21, transcendentals=0),
    )(
        *(
            pltpu.with_memory_space_constraint(operand, pltpu.HBM)
            for operand in (
                cholesky_a, cholesky_b.reshape(768, 256), amplitudes.reshape(256, 256),
                virtual_a.reshape(1, 16), virtual_b.reshape(1, 12), pair_energy.reshape(1, 256),
            )
        )
    )
    residual = other_terms + ladder.reshape(12, 16, 256).transpose(1, 0, 2)
    return (residual, residual / divisor.reshape(12, 16, 256).transpose(1, 0, 2))


def solution(mesh):
    return jax.shard_map(
        shards,
        mesh=mesh,
        in_specs=(
            P(("rep", "ab"), None, "ij"),
            P("rep", None, "ij"),
            P("ab", None, "ij"),
            P(("rep", "ab"), None, "ij"),
            P(("rep", "ab")),
            P("rep"),
            P("ij"),
        ),
        out_specs=(P(("rep", "ab"), None, "ij"), P(("rep", "ab"), None, "ij")),
        check_vma=False,
    )
```

```python
import jax
import jax.numpy as jnp
from jax import lax
from jax.experimental import pallas as pl
from jax.experimental.pallas import tpu as pltpu
from jax.sharding import PartitionSpec as P

MESH = pl.DeviceIdType.MESH
BF16, F32 = jnp.bfloat16, jnp.float32
RING = 8
T_HOPS = {1: 3, -1: 4}
PIECES = 4
LONG = {1: (0, 1), -1: (2, 3)}
SHORT = {1: (2, 3), -1: (0, 1)}
N_RECV, N_SEND = 42, 7


SLOTS = {
    key: i for i, key in enumerate(
        (s, stage, piece) for s in (1, -1) for stage in range(4) for piece in LONG[s] + (SHORT[s] if stage < 3 else ())
    )
}


REUSED = {(0, ("z", -1, 4, piece)): ("z", -1, 1, piece) for piece in range(PIECES)}
REUSED |= {(0, ("far", 4, half)): ("far", 0, half) for half in range(2)}
REUSED |= {(0, "g early"): "t"}


def dot(a, b, dims):
    return lax.dot_general(a, b, (dims, ((), ())), preferred_element_type=F32)


def rotation(pieces, ways=(1, -1)):
    return [(s, pieces[s][i]) for i in range(PIECES // 2) for s in ways]


def kernel(a_hbm, b_hbm, t_hbm, va_hbm, vb_hbm, pe_hbm, out_ref, div_ref,
           va_ref, vb_ref, pe_ref, a_in, a_all, b_all, part, part_0, rs_in, rs_out, gath, t_all,
           send_sem, recv_sem, load_sem, go_sem, ready_sem):
    ab, ij, lo = lax.axis_index("ab"), lax.axis_index("ij"), lax.axis_index("rep")
    z, hi = ab // 2, ab % 2
    y, core = ij // 2, ij % 2
    sibling = (ab, y * 2 + 1 - core, lo)
    y_next = {s: (ab, ((y + s + RING) % RING) * 2 + core, lo) for s in (1, -1)}
    z_hop = {s: (((z + s + RING) % RING) * 2 + hi, ij, lo) for s in (1, -1)}
    x_far = (z * 2 + 1 - hi, ij, 1 - lo)
    x_near = (ab, ij, 1 - lo)
    x_far_sibling = (z * 2 + 1 - hi, y * 2 + 1 - core, 1 - lo)
    x_near_sibling = (ab, y * 2 + 1 - core, 1 - lo)

    numbers = ({}, {})

    def recv_of(to, name):
        if isinstance(name, tuple) and name[0] == "g":
            name = ("rs", *name[1:])
        name = REUSED.get((to, name), name)
        return recv_sem.at[numbers[to].setdefault(name, len(numbers[to]))]

    def send(to, name, src, dst, device, group):
        pltpu.make_async_remote_copy(
            src_ref=src, dst_ref=dst, send_sem=send_sem.at[group], recv_sem=recv_of(to, name),
            device_id=device, device_id_type=MESH,
        ).start()

    def arrived(to, name, ref):
        pltpu.make_async_remote_copy(
            src_ref=ref, dst_ref=ref, send_sem=send_sem.at[0], recv_sem=recv_of(to, name),
            device_id=sibling, device_id_type=MESH,
        ).wait_recv()

    def sent(group, ref):
        pltpu.make_async_remote_copy(
            src_ref=ref, dst_ref=ref, send_sem=send_sem.at[group], recv_sem=recv_sem.at[0],
            device_id=sibling, device_id_type=MESH,
        ).wait_send()

    load_a = pltpu.make_async_copy(a_hbm, a_in, load_sem.at[0])
    load_b = pltpu.make_async_copy(b_hbm, b_all, load_sem.at[1])
    load_t = pltpu.make_async_copy(t_hbm, t_all.at[core, ab], load_sem.at[2])
    loads_small = [
        pltpu.make_async_copy(src, dst, load_sem.at[3 + i])
        for i, (src, dst) in enumerate(((va_hbm, va_ref), (vb_hbm, vb_ref), (pe_hbm, pe_ref)))
    ]

    barrier = pltpu.get_barrier_semaphore()

    def enter(friends):
        for friend in friends:
            pl.semaphore_signal(barrier, inc=1, device_id=friend, device_id_type=MESH)
        for load in (load_a, load_b, load_t, *loads_small):
            load.start()

    def swap():
        row = lax.broadcasted_iota(jnp.int32, (256, 256), 0)
        column = lax.broadcasted_iota(jnp.int32, (256, 256), 1)
        return jnp.where(column == (row % 16) * 16 + row // 16, 1.0, 0.0).astype(BF16)

    def reorder(k, matrix):
        block = ((y + 4) // 2 + k) % 4
        rows = a_in[:, pl.ds(pl.multiple_of(block * 16, 16), 16), :].reshape(256, 256)
        place = pl.ds(pl.multiple_of(block * 256, 256), 256)
        a_all[place, :] = dot(matrix, rows, ((1,), (0,))).astype(BF16)

    def chunk_rows(offset):
        return pl.ds(pl.multiple_of(((y + offset + RING) % RING) * 128, 128), 128)

    def piece_rows(offset, piece):
        return pl.ds(pl.multiple_of(((y + offset + RING) % RING) * 128 + piece * 32, 32), 32)

    def products(ref, *offsets):
        left = jnp.concatenate([a_all[chunk_rows(offset), :] for offset in offsets], axis=0)
        value = dot(left, b_all[...], ((1,), (1,))).astype(ref.dtype)
        for i, offset in enumerate(offsets):
            ref[chunk_rows(offset), :] = value[i * 128:(i + 1) * 128]

    def divisor():
        for load in loads_small:
            load.wait()
        eye = lax.broadcasted_iota(jnp.int32, (16, 16), 0) == lax.broadcasted_iota(jnp.int32, (16, 16), 1)
        va = jnp.sum(jnp.where(eye, jnp.broadcast_to(va_ref[...], (16, 16)), 0.0), axis=1, keepdims=True)
        for b in range(12):
            div_ref[b * 16:(b + 1) * 16, :] = (va + vb_ref[0:1, b:b + 1]) - pe_ref[...]

    far_y = (y + 4) % RING
    ahead = (far_y - z + 2 + RING) % RING
    skipped = jnp.where(ahead < 5, ahead, 2)
    slabs_early = [(z - 2 + k + jnp.where(k >= skipped, 1, 0) + RING) % RING for k in range(4)]
    slabs_late = [(z + offset) % RING for offset in (3, 5, 4)]
    slab_between = jnp.where(ahead < 5, far_y, z)

    def ladder_of(slabs, half):
        left = [gath[slab, 2 * half + p] for slab in slabs for p in range(PIECES // 2)]
        right = [t_all[core, 2 * slab + half] for slab in slabs]
        return dot(jnp.concatenate(left, axis=1), jnp.concatenate(right, axis=0), ((1,), (0,)))

    def ladder(slabs):
        total = None
        for slab in slabs:
            left = jnp.concatenate([gath[slab, p] for p in range(PIECES)], axis=1)
            right = t_all[core, pl.ds(2 * slab, 2)].reshape(512, 256)
            product = dot(left, right, ((1,), (0,)))
            total = product if total is None else total + product
        return total

    def amplitudes(first_plane):
        friends = (*z_hop.values(), x_far, x_near)
        enter((sibling, *friends))

        def hand_products(*offsets):
            products(part_0, *offsets)
            if offsets == (4,):
                pl.semaphore_wait(go_sem, 1)
                for _, piece in rotation(LONG):
                    ref = part_0.at[piece_rows(4, piece)]
                    send(1, ("p", 4, piece), ref, ref, sibling, 0)
                return
            for offset in offsets:
                ref = part_0.at[chunk_rows(offset)]
                send(1, ("p", offsets[0]), ref, ref, sibling, 0)

        def own(offset):
            return ((z + offset + RING) % RING) * 2 + hi

        def other(offset):
            return ((z + offset + RING) % RING) * 2 + 1 - hi

        def half_rows(half):
            return pl.ds(half * 128, 128)

        def piece_of(slab, piece):
            return t_all.at[piece % 2, slab, half_rows(piece // 2)]

        def z_send(s, distance, piece):
            ref = piece_of(own(-s * (distance - 1)), piece)
            send(0, ("z", s, distance, piece), ref, ref, z_hop[s], 2)

        def far_send(offset, piece):
            ref = piece_of(own(offset), piece)

            def go():
                send(0, ("far", offset, piece // 2), ref, ref, x_far, 3)

            if offset != 4:
                pl.when(lo == piece % 2)(go)
            elif piece % 2:
                send(1, "t last", ref, ref, x_far_sibling, 3)
            else:
                go()

        def z_arrived(s, distance, piece):
            ref = piece_of(own(-s * distance), piece)
            arrived(0, ("z", s, distance, piece), ref)
            if distance < T_HOPS[s]:
                z_send(s, distance + 1, piece)
            far_send(4 if distance == 4 else -s * distance, piece)
            if piece % 2:
                send(1, "t" if distance < 3 else "t own", ref, ref, sibling, 5)

        def near(offset, half):
            ref = t_all.at[1 - lo, other(offset), half_rows(half)]
            arrived(0, ("far", offset, half), ref)
            late = " last" if abs(offset) == 3 else ""

            def column_0():
                send(0, "near" + late, ref, ref, x_near, 4)

            def column_1():
                send(1, "t" + late, ref, ref, x_near_sibling, 4)
                send(1, "t" + late, ref, ref, sibling, 6)

            pl.when(lo == 1)(column_0)
            pl.when(lo == 0)(column_1)

        def more_products():
            for k in (1, 3, 2):
                reorder(k, matrix)
            hand_products(3, -3)
            hand_products(2, -2)

        def start_column(col):
            for half in range(2):
                for s in (1, -1):
                    z_send(s, 1, 2 * half + col)
            for half in range(2):
                far_send(0, 2 * half + col)

        def start_amplitudes():
            pl.semaphore_wait(barrier, len(friends))
            load_t.wait()
            start_column(0)

        def second_column():
            arrived(0, "t", t_all.at[1, ab])
            start_column(1)
            for friend in (x_near, x_far):
                pl.semaphore_signal(ready_sem, inc=1, device_id=friend, device_id_type=MESH)

        matrix = swap()
        if not first_plane:
            start_amplitudes()
        load_a.wait()
        reorder(0, matrix)
        load_b.wait()
        hand_products(4)
        if first_plane:
            more_products()
            start_amplitudes()
        second_column()
        if not first_plane:
            more_products()
        hand_products(1, -1)
        hand_products(0)
        divisor()

        turns = (0, 2, 1, 3)

        def both(distance):
            for piece in turns:
                for s in (1, -1):
                    z_arrived(s, distance, piece)

        def near_both(distance, half):
            for s in (1, -1):
                near(-s * distance, half)

        both(1)
        pl.semaphore_wait(ready_sem, 2)
        for half in range(2):
            near(0, half)
        for distance in (2, 3):
            both(distance)
            for half in range(2):
                near_both(distance - 1, half)
        for piece in (0, 1):
            z_arrived(-1, 4, piece)
        near_both(3, 0)
        for piece in (3, 2):
            z_arrived(-1, 4, piece)
        near_both(3, 1)
        pl.when(lo == 0)(lambda: arrived(0, "near", t_all.at[0, 0:5]))
        arrived(0, "g early", gath.at[0:7])
        out_ref[...] = ladder(slabs_early)
        arrived(0, "g last", gath.at[0])
        out_ref[...] += ladder([slab_between]) + ladder_of(slabs_late, hi)
        for half in range(2):
            arrived(0, ("far", 4, half), t_all.at[0, other(4), half_rows(half)])
        pl.when(lo == 0)(lambda: arrived(0, "near last", t_all.at[0, 0:2]))
        out_ref[...] += ladder_of(slabs_late, 1 - hi)

        sent(0, part_0)
        sent(2, t_all.at[0, 0:14])
        sent(3, t_all.at[0, 0:9])
        sent(4, t_all.at[0, 0:7])
        sent(5, t_all.at[0, 0:7])
        pl.when(lo == 0)(lambda: sent(6, t_all.at[0, 0:7]))

    def integrals(ways):
        enter(y_next.values())
        pl.semaphore_wait(barrier, 3)
        pl.semaphore_signal(go_sem, inc=1, device_id=sibling, device_id_type=MESH)
        send(0, "t", t_hbm, t_all.at[1, ab], sibling, 0)

        def own_part(offset, piece):
            rows = piece_rows(offset, piece)
            return part[rows, :] + part_0[rows, :].astype(F32)

        def received(s, stage, piece):
            slot = SLOTS[s, stage, piece]
            arrived(1, ("rs", s, stage, piece), rs_in.at[slot])
            return rs_in[slot].astype(F32)

        def rs_send(s, stage, piece):
            value = own_part(s * ((4 if piece in LONG[s] else 3) - stage), piece)
            if stage:
                value = value + received(s, stage - 1, piece)
            slot = SLOTS[s, stage, piece]
            rs_out[slot] = value.astype(BF16)
            send(1, ("rs", s, stage, piece), rs_out.at[slot], rs_in.at[slot], y_next[s], 1)

        def rs_stage(stage, pieces):
            for s, piece in rotation(pieces, ways):
                rs_send(s, stage, piece)

        matrix = swap()
        load_a.wait()
        for k in range(4):
            reorder(k, matrix)
        load_b.wait()
        products(part, 4)
        products(part, 3, -3)
        products(part, 2, -2)
        for s, piece in rotation(LONG, ways):
            arrived(1, ("p", 4, piece), part_0.at[0:32])
            rs_send(s, 0, piece)
        arrived(1, ("p", 3), part_0.at[0:256])
        rs_stage(0, SHORT)
        products(part, 1, -1)
        products(part, 0)
        rs_stage(1, LONG)
        arrived(1, ("p", 2), part_0.at[0:256])
        rs_stage(1, SHORT)
        rs_stage(2, LONG)
        arrived(1, ("p", 1), part_0.at[0:256])
        rs_stage(2, SHORT)
        rs_stage(3, LONG)
        arrived(1, ("p", 0), part_0.at[0:128])

        def slab_of(offset):
            return (y + offset + RING) % RING

        def g_send(s, stage, piece):
            ref = gath.at[slab_of(-s * stage), piece]
            send(1, ("g", s, stage, piece), ref, ref, y_next[s], 2)

        def g_arrived(s, stage, piece):
            offset = -s * (stage + 1)
            arrived(1, ("g", s, stage, piece), gath.at[slab_of(offset), piece])
            if stage < (3 if piece in LONG[s] else 2):
                g_send(s, stage + 1, piece)
            g_hand(offset, piece)

        def g_hand(offset, piece):
            ref = gath.at[slab_of(offset), piece]
            send(0, "g last" if abs(offset) == 4 else "g early", ref, ref, sibling, 3)

        for way, piece in rotation(LONG, ways):
            value = own_part(0, piece)
            for s in (1, -1):
                value = value + received(s, 3 if piece in LONG[s] else 2, piece)
            for b in range(12):
                block = jnp.concatenate([value[c * 16:(c + 1) * 16, b * 64:(b + 1) * 64] for c in range(2)], axis=1)
                gath[y, piece, b * 16:(b + 1) * 16, :] = block.astype(BF16)
            g_send(way, 0, piece)
        for s, piece in rotation(SHORT, ways):
            g_send(s, 0, piece)
        for piece in range(PIECES):
            g_hand(0, piece)
        for stage in range(3):
            for pieces in (LONG, SHORT):
                for s, piece in rotation(pieces, ways):
                    g_arrived(s, stage, piece)
        divisor()
        load_t.wait()
        arrived(1, "t", t_all.at[1, 0:9])
        out_ref[...] = ladder(slabs_early)
        for s, piece in rotation(LONG, ways):
            g_arrived(s, 3, piece)
        arrived(1, "t own", t_all.at[1, 0:3])
        out_ref[...] += ladder([slab_between]) + ladder_of(slabs_late, hi)
        arrived(1, "t last", t_all.at[1, 0:3])
        out_ref[...] += ladder_of(slabs_late, 1 - hi)

        sent(0, t_all.at[1, 0])
        sent(1, rs_out)
        sent(2, gath.at[0:7])
        sent(3, gath)

    pl.when((core == 1) & (y % 4 < 2))(lambda: integrals((-1, 1)))
    pl.when((core == 1) & (y % 4 >= 2))(lambda: integrals((1, -1)))
    pl.when((core == 0) & (z == 0))(lambda: amplitudes(True))
    pl.when((core == 0) & (z > 0))(lambda: amplitudes(False))
    assert max(map(len, numbers)) <= N_RECV


def shards(cholesky_a, cholesky_b, amplitudes, other_terms, virtual_a, virtual_b, pair_energy):
    hbm = pl.BlockSpec(memory_space=pltpu.HBM)
    vmem = pl.BlockSpec(memory_space=pltpu.VMEM)
    result = jax.ShapeDtypeStruct((192, 256), F32)
    ladder, divisor = pl.pallas_call(
        kernel,
        out_shape=(result, result),
        in_specs=[hbm] * 6,
        out_specs=(vmem, vmem),
        scratch_shapes=[
            pltpu.VMEM((1, 16), F32),
            pltpu.VMEM((1, 12), F32),
            pltpu.VMEM((1, 256), F32),
            pltpu.VMEM((16, 64, 256), BF16),
            pltpu.VMEM((1024, 256), BF16),
            pltpu.VMEM((768, 256), BF16),
            pltpu.VMEM((1024, 768), F32),
            pltpu.VMEM((1024, 768), BF16),
            pltpu.VMEM((28, 32, 768), BF16),
            pltpu.VMEM((28, 32, 768), BF16),
            pltpu.VMEM((8, PIECES, 192, 128), BF16),
            pltpu.VMEM((2, 16, 256, 256), BF16),
            pltpu.SemaphoreType.DMA((N_SEND,)),
            pltpu.SemaphoreType.DMA((N_RECV,)),
            pltpu.SemaphoreType.DMA((6,)),
            pltpu.SemaphoreType.REGULAR,
            pltpu.SemaphoreType.REGULAR,
        ],
        compiler_params=pltpu.CompilerParams(
            collective_id=0, has_side_effects=True, vmem_limit_bytes=40 * 2**20
        ),
        cost_estimate=pl.CostEstimate(flops=2 * 1024 * 512 * 768 + 2 * 192 * 4096 * 256, bytes_accessed=2**21, transcendentals=0),
    )(
        *(
            pltpu.with_memory_space_constraint(operand, pltpu.HBM)
            for operand in (
                cholesky_a, cholesky_b.reshape(768, 256), amplitudes.reshape(256, 256),
                virtual_a.reshape(1, 16), virtual_b.reshape(1, 12), pair_energy.reshape(1, 256),
            )
        )
    )
    residual = other_terms + ladder.reshape(12, 16, 256).transpose(1, 0, 2)
    return (residual, residual / divisor.reshape(12, 16, 256).transpose(1, 0, 2))


def solution(mesh):
    return jax.shard_map(
        shards,
        mesh=mesh,
        in_specs=(
            P(("rep", "ab"), None, "ij"),
            P("rep", None, "ij"),
            P("ab", None, "ij"),
            P(("rep", "ab"), None, "ij"),
            P(("rep", "ab")),
            P("rep"),
            P("ij"),
        ),
        out_specs=(P(("rep", "ab"), None, "ij"), P(("rep", "ab"), None, "ij")),
        check_vma=False,
    )
```

```python
import jax
import jax.numpy as jnp
from jax import lax
from jax.experimental import pallas as pl
from jax.experimental.pallas import tpu as pltpu
from jax.sharding import PartitionSpec as P

MESH = pl.DeviceIdType.MESH
BF16, F32 = jnp.bfloat16, jnp.float32
RING = 8
T_HOPS = {1: 3, -1: 4}
PIECES = 4
LONG = {1: (0, 1), -1: (2, 3)}
SHORT = {1: (2, 3), -1: (0, 1)}
N_RECV, N_SEND = 42, 7


SLOTS = {
    key: i for i, key in enumerate(
        (s, stage, piece) for s in (1, -1) for stage in range(4) for piece in LONG[s] + (SHORT[s] if stage < 3 else ())
    )
}


REUSED = {(0, ("z", -1, 4, piece)): ("z", -1, 1, piece) for piece in range(PIECES)}
REUSED |= {(0, ("far", 4, half)): ("far", 0, half) for half in range(2)}
REUSED |= {(0, "g early"): "t"}


def dot(a, b, dims):
    return lax.dot_general(a, b, (dims, ((), ())), preferred_element_type=F32)


def rotation(pieces, ways=(1, -1)):
    return [(s, pieces[s][i]) for i in range(PIECES // 2) for s in ways]


def kernel(a_hbm, b_hbm, t_hbm, va_hbm, vb_hbm, pe_hbm, out_ref, div_ref,
           va_ref, vb_ref, pe_ref, a_in, a_all, b_all, part, part_0, rs_in, rs_out, gath, t_all,
           send_sem, recv_sem, load_sem, go_sem, ready_sem):
    ab, ij, lo = lax.axis_index("ab"), lax.axis_index("ij"), lax.axis_index("rep")
    z, hi = ab // 2, ab % 2
    y, core = ij // 2, ij % 2
    sibling = (ab, y * 2 + 1 - core, lo)
    y_next = {s: (ab, ((y + s + RING) % RING) * 2 + core, lo) for s in (1, -1)}
    z_hop = {s: (((z + s + RING) % RING) * 2 + hi, ij, lo) for s in (1, -1)}
    x_far = (z * 2 + 1 - hi, ij, 1 - lo)
    x_near = (ab, ij, 1 - lo)
    x_far_sibling = (z * 2 + 1 - hi, y * 2 + 1 - core, 1 - lo)
    x_near_sibling = (ab, y * 2 + 1 - core, 1 - lo)

    numbers = ({}, {})

    def recv_of(to, name):
        if isinstance(name, tuple) and name[0] == "g":
            name = ("rs", *name[1:])
        name = REUSED.get((to, name), name)
        return recv_sem.at[numbers[to].setdefault(name, len(numbers[to]))]

    def send(to, name, src, dst, device, group):
        pltpu.make_async_remote_copy(
            src_ref=src, dst_ref=dst, send_sem=send_sem.at[group], recv_sem=recv_of(to, name),
            device_id=device, device_id_type=MESH,
        ).start()

    def arrived(to, name, ref):
        pltpu.make_async_remote_copy(
            src_ref=ref, dst_ref=ref, send_sem=send_sem.at[0], recv_sem=recv_of(to, name),
            device_id=sibling, device_id_type=MESH,
        ).wait_recv()

    def sent(group, ref):
        pltpu.make_async_remote_copy(
            src_ref=ref, dst_ref=ref, send_sem=send_sem.at[group], recv_sem=recv_sem.at[0],
            device_id=sibling, device_id_type=MESH,
        ).wait_send()

    load_a = pltpu.make_async_copy(a_hbm, a_in, load_sem.at[0])
    load_b = pltpu.make_async_copy(b_hbm, b_all, load_sem.at[1])
    load_t = pltpu.make_async_copy(t_hbm, t_all.at[core, ab], load_sem.at[2])
    loads_small = [
        pltpu.make_async_copy(src, dst, load_sem.at[3 + i])
        for i, (src, dst) in enumerate(((va_hbm, va_ref), (vb_hbm, vb_ref), (pe_hbm, pe_ref)))
    ]

    barrier = pltpu.get_barrier_semaphore()

    def enter(friends):
        for friend in friends:
            pl.semaphore_signal(barrier, inc=1, device_id=friend, device_id_type=MESH)
        for load in (load_t, load_a, load_b, *loads_small):
            load.start()

    def swap():
        row = lax.broadcasted_iota(jnp.int32, (256, 256), 0)
        column = lax.broadcasted_iota(jnp.int32, (256, 256), 1)
        return jnp.where(column == (row % 16) * 16 + row // 16, 1.0, 0.0).astype(BF16)

    def reorder(k, matrix):
        block = ((y + 4) // 2 + k) % 4
        rows = a_in[:, pl.ds(pl.multiple_of(block * 16, 16), 16), :].reshape(256, 256)
        place = pl.ds(pl.multiple_of(block * 256, 256), 256)
        a_all[place, :] = dot(matrix, rows, ((1,), (0,))).astype(BF16)

    def chunk_rows(offset):
        return pl.ds(pl.multiple_of(((y + offset + RING) % RING) * 128, 128), 128)

    def piece_rows(offset, piece):
        return pl.ds(pl.multiple_of(((y + offset + RING) % RING) * 128 + piece * 32, 32), 32)

    def products(ref, *offsets):
        left = jnp.concatenate([a_all[chunk_rows(offset), :] for offset in offsets], axis=0)
        value = dot(left, b_all[...], ((1,), (1,))).astype(ref.dtype)
        for i, offset in enumerate(offsets):
            ref[chunk_rows(offset), :] = value[i * 128:(i + 1) * 128]

    def divisor():
        for load in loads_small:
            load.wait()
        eye = lax.broadcasted_iota(jnp.int32, (16, 16), 0) == lax.broadcasted_iota(jnp.int32, (16, 16), 1)
        va = jnp.sum(jnp.where(eye, jnp.broadcast_to(va_ref[...], (16, 16)), 0.0), axis=1, keepdims=True)
        for b in range(12):
            div_ref[b * 16:(b + 1) * 16, :] = (va + vb_ref[0:1, b:b + 1]) - pe_ref[...]

    far_y = (y + 4) % RING
    ahead = (far_y - z + 2 + RING) % RING
    skipped = jnp.where(ahead < 5, ahead, 2)
    slabs_early = [(z - 2 + k + jnp.where(k >= skipped, 1, 0) + RING) % RING for k in range(4)]
    slabs_late = [(z + offset) % RING for offset in (3, 5, 4)]
    slab_between = jnp.where(ahead < 5, far_y, z)

    def ladder_of(slabs, half):
        left = [gath[slab, 2 * half + p] for slab in slabs for p in range(PIECES // 2)]
        right = [t_all[core, 2 * slab + half] for slab in slabs]
        return dot(jnp.concatenate(left, axis=1), jnp.concatenate(right, axis=0), ((1,), (0,)))

    def ladder(slabs):
        total = None
        for slab in slabs:
            left = jnp.concatenate([gath[slab, p] for p in range(PIECES)], axis=1)
            right = t_all[core, pl.ds(2 * slab, 2)].reshape(512, 256)
            product = dot(left, right, ((1,), (0,)))
            total = product if total is None else total + product
        return total

    def amplitudes(first_plane):
        friends = (*z_hop.values(), x_far, x_near)
        enter((*friends, sibling))

        def hand_products(*offsets):
            products(part_0, *offsets)
            if offsets == (4,):
                pl.semaphore_wait(go_sem, 1)
                for _, piece in rotation(LONG):
                    ref = part_0.at[piece_rows(4, piece)]
                    send(1, ("p", 4, piece), ref, ref, sibling, 0)
                return
            for offset in offsets:
                ref = part_0.at[chunk_rows(offset)]
                send(1, ("p", offsets[0]), ref, ref, sibling, 0)

        def own(offset):
            return ((z + offset + RING) % RING) * 2 + hi

        def other(offset):
            return ((z + offset + RING) % RING) * 2 + 1 - hi

        def half_rows(half):
            return pl.ds(half * 128, 128)

        def piece_of(slab, piece):
            return t_all.at[piece % 2, slab, half_rows(piece // 2)]

        def z_send(s, distance, piece):
            ref = piece_of(own(-s * (distance - 1)), piece)
            send(0, ("z", s, distance, piece), ref, ref, z_hop[s], 2)

        def far_send(offset, piece):
            ref = piece_of(own(offset), piece)

            def go():
                send(0, ("far", offset, piece // 2), ref, ref, x_far, 3)

            if offset != 4:
                pl.when(lo == piece % 2)(go)
            elif piece % 2:
                send(1, "t last", ref, ref, x_far_sibling, 3)
            else:
                go()

        def z_arrived(s, distance, piece):
            ref = piece_of(own(-s * distance), piece)
            arrived(0, ("z", s, distance, piece), ref)
            if distance < T_HOPS[s]:
                z_send(s, distance + 1, piece)
            far_send(4 if distance == 4 else -s * distance, piece)
            if piece % 2:
                send(1, "t" if distance < 3 else "t own", ref, ref, sibling, 5)

        def near(offset, half):
            ref = t_all.at[1 - lo, other(offset), half_rows(half)]
            arrived(0, ("far", offset, half), ref)
            late = " last" if abs(offset) == 3 else ""

            def column_0():
                send(0, "near" + late, ref, ref, x_near, 4)

            def column_1():
                send(1, "t" + late, ref, ref, x_near_sibling, 4)
                send(1, "t" + late, ref, ref, sibling, 6)

            pl.when(lo == 1)(column_0)
            pl.when(lo == 0)(column_1)

        def more_products():
            for k in (1, 3, 2):
                reorder(k, matrix)
            hand_products(3, -3)
            hand_products(2, -2)

        def start_column(col):
            for half in range(2):
                for s in (1, -1):
                    z_send(s, 1, 2 * half + col)
            for half in range(2):
                far_send(0, 2 * half + col)

        def start_amplitudes():
            pl.semaphore_wait(barrier, len(friends))
            load_t.wait()
            start_column(0)

        def second_column():
            arrived(0, "t", t_all.at[1, ab])
            start_column(1)
            for friend in (x_near, x_far):
                pl.semaphore_signal(ready_sem, inc=1, device_id=friend, device_id_type=MESH)

        matrix = swap()
        if not first_plane:
            start_amplitudes()
        load_a.wait()
        reorder(0, matrix)
        load_b.wait()
        hand_products(4)
        if first_plane:
            more_products()
            start_amplitudes()
        second_column()
        if not first_plane:
            more_products()
        hand_products(1, -1)
        hand_products(0)
        divisor()

        turns = (0, 2, 1, 3)

        def both(distance):
            for piece in turns:
                for s in (1, -1):
                    z_arrived(s, distance, piece)

        def near_both(distance, half):
            for s in (1, -1):
                near(-s * distance, half)

        both(1)
        pl.semaphore_wait(ready_sem, 2)
        for half in range(2):
            near(0, half)
        for distance in (2, 3):
            both(distance)
            for half in range(2):
                near_both(distance - 1, half)
        for piece in (0, 1):
            z_arrived(-1, 4, piece)
        near_both(3, 0)
        for piece in (3, 2):
            z_arrived(-1, 4, piece)
        near_both(3, 1)
        pl.when(lo == 0)(lambda: arrived(0, "near", t_all.at[0, 0:5]))
        arrived(0, "g early", gath.at[0:7])
        out_ref[...] = ladder(slabs_early)
        arrived(0, "g last", gath.at[0])
        out_ref[...] += ladder([slab_between]) + ladder_of(slabs_late, hi)
        for half in range(2):
            arrived(0, ("far", 4, half), t_all.at[0, other(4), half_rows(half)])
        pl.when(lo == 0)(lambda: arrived(0, "near last", t_all.at[0, 0:2]))
        out_ref[...] += ladder_of(slabs_late, 1 - hi)

        sent(0, part_0)
        sent(2, t_all.at[0, 0:14])
        sent(3, t_all.at[0, 0:9])
        sent(4, t_all.at[0, 0:7])
        sent(5, t_all.at[0, 0:7])
        pl.when(lo == 0)(lambda: sent(6, t_all.at[0, 0:7]))

    def integrals(ways):
        enter(y_next.values())
        pl.semaphore_wait(barrier, 3)
        pl.semaphore_signal(go_sem, inc=1, device_id=sibling, device_id_type=MESH)
        send(0, "t", t_hbm, t_all.at[1, ab], sibling, 0)

        def own_part(offset, piece):
            rows = piece_rows(offset, piece)
            return part[rows, :] + part_0[rows, :].astype(F32)

        def received(s, stage, piece):
            slot = SLOTS[s, stage, piece]
            arrived(1, ("rs", s, stage, piece), rs_in.at[slot])
            return rs_in[slot].astype(F32)

        def rs_send(s, stage, piece):
            value = own_part(s * ((4 if piece in LONG[s] else 3) - stage), piece)
            if stage:
                value = value + received(s, stage - 1, piece)
            slot = SLOTS[s, stage, piece]
            rs_out[slot] = value.astype(BF16)
            send(1, ("rs", s, stage, piece), rs_out.at[slot], rs_in.at[slot], y_next[s], 1)

        def rs_stage(stage, pieces):
            for s, piece in rotation(pieces, ways):
                rs_send(s, stage, piece)

        matrix = swap()
        load_a.wait()
        for k in range(4):
            reorder(k, matrix)
        load_b.wait()
        products(part, 4)
        products(part, 3, -3)
        products(part, 2, -2)
        for s, piece in rotation(LONG, ways):
            arrived(1, ("p", 4, piece), part_0.at[0:32])
            rs_send(s, 0, piece)
        arrived(1, ("p", 3), part_0.at[0:256])
        rs_stage(0, SHORT)
        products(part, 1, -1)
        products(part, 0)
        rs_stage(1, LONG)
        arrived(1, ("p", 2), part_0.at[0:256])
        rs_stage(1, SHORT)
        rs_stage(2, LONG)
        arrived(1, ("p", 1), part_0.at[0:256])
        rs_stage(2, SHORT)
        rs_stage(3, LONG)
        arrived(1, ("p", 0), part_0.at[0:128])

        def slab_of(offset):
            return (y + offset + RING) % RING

        def g_send(s, stage, piece):
            ref = gath.at[slab_of(-s * stage), piece]
            send(1, ("g", s, stage, piece), ref, ref, y_next[s], 2)

        def g_arrived(s, stage, piece):
            offset = -s * (stage + 1)
            arrived(1, ("g", s, stage, piece), gath.at[slab_of(offset), piece])
            if stage < (3 if piece in LONG[s] else 2):
                g_send(s, stage + 1, piece)
            g_hand(offset, piece)

        def g_hand(offset, piece):
            ref = gath.at[slab_of(offset), piece]
            send(0, "g last" if abs(offset) == 4 else "g early", ref, ref, sibling, 3)

        for way, piece in rotation(LONG, ways):
            value = own_part(0, piece)
            for s in (1, -1):
                value = value + received(s, 3 if piece in LONG[s] else 2, piece)
            for b in range(12):
                block = jnp.concatenate([value[c * 16:(c + 1) * 16, b * 64:(b + 1) * 64] for c in range(2)], axis=1)
                gath[y, piece, b * 16:(b + 1) * 16, :] = block.astype(BF16)
            g_send(way, 0, piece)
        for s, piece in rotation(SHORT, ways):
            g_send(s, 0, piece)
        for piece in range(PIECES):
            g_hand(0, piece)
        for stage in range(3):
            for pieces in (LONG, SHORT):
                for s, piece in rotation(pieces, ways):
                    g_arrived(s, stage, piece)
        divisor()
        load_t.wait()
        arrived(1, "t", t_all.at[1, 0:9])
        out_ref[...] = ladder(slabs_early)
        for s, piece in rotation(LONG, ways):
            g_arrived(s, 3, piece)
        arrived(1, "t own", t_all.at[1, 0:3])
        out_ref[...] += ladder([slab_between]) + ladder_of(slabs_late, hi)
        arrived(1, "t last", t_all.at[1, 0:3])
        out_ref[...] += ladder_of(slabs_late, 1 - hi)

        sent(0, t_all.at[1, 0])
        sent(1, rs_out)
        sent(2, gath.at[0:7])
        sent(3, gath)

    pl.when((core == 1) & (y % 4 < 2))(lambda: integrals((-1, 1)))
    pl.when((core == 1) & (y % 4 >= 2))(lambda: integrals((1, -1)))
    pl.when((core == 0) & (z == 0))(lambda: amplitudes(True))
    pl.when((core == 0) & (z > 0))(lambda: amplitudes(False))
    assert max(map(len, numbers)) <= N_RECV


def shards(cholesky_a, cholesky_b, amplitudes, other_terms, virtual_a, virtual_b, pair_energy):
    hbm = pl.BlockSpec(memory_space=pltpu.HBM)
    vmem = pl.BlockSpec(memory_space=pltpu.VMEM)
    result = jax.ShapeDtypeStruct((192, 256), F32)
    ladder, divisor = pl.pallas_call(
        kernel,
        out_shape=(result, result),
        in_specs=[hbm] * 6,
        out_specs=(vmem, vmem),
        scratch_shapes=[
            pltpu.VMEM((1, 16), F32),
            pltpu.VMEM((1, 12), F32),
            pltpu.VMEM((1, 256), F32),
            pltpu.VMEM((16, 64, 256), BF16),
            pltpu.VMEM((1024, 256), BF16),
            pltpu.VMEM((768, 256), BF16),
            pltpu.VMEM((1024, 768), F32),
            pltpu.VMEM((1024, 768), BF16),
            pltpu.VMEM((28, 32, 768), BF16),
            pltpu.VMEM((28, 32, 768), BF16),
            pltpu.VMEM((8, PIECES, 192, 128), BF16),
            pltpu.VMEM((2, 16, 256, 256), BF16),
            pltpu.SemaphoreType.DMA((N_SEND,)),
            pltpu.SemaphoreType.DMA((N_RECV,)),
            pltpu.SemaphoreType.DMA((6,)),
            pltpu.SemaphoreType.REGULAR,
            pltpu.SemaphoreType.REGULAR,
        ],
        compiler_params=pltpu.CompilerParams(
            collective_id=0, has_side_effects=True, vmem_limit_bytes=40 * 2**20
        ),
        cost_estimate=pl.CostEstimate(flops=2 * 1024 * 512 * 768 + 2 * 192 * 4096 * 256, bytes_accessed=2**21, transcendentals=0),
    )(
        *(
            pltpu.with_memory_space_constraint(operand, pltpu.HBM)
            for operand in (
                cholesky_a, cholesky_b.reshape(768, 256), amplitudes.reshape(256, 256),
                virtual_a.reshape(1, 16), virtual_b.reshape(1, 12), pair_energy.reshape(1, 256),
            )
        )
    )
    residual = other_terms + ladder.reshape(12, 16, 256).transpose(1, 0, 2)
    return (residual, residual / divisor.reshape(12, 16, 256).transpose(1, 0, 2))


def solution(mesh):
    return jax.shard_map(
        shards,
        mesh=mesh,
        in_specs=(
            P(("rep", "ab"), None, "ij"),
            P("rep", None, "ij"),
            P("ab", None, "ij"),
            P(("rep", "ab"), None, "ij"),
            P(("rep", "ab")),
            P("rep"),
            P("ij"),
        ),
        out_specs=(P(("rep", "ab"), None, "ij"), P(("rep", "ab"), None, "ij")),
        check_vma=False,
    )
```
